32 devices in a mesh: groups: 2 (over x), gx: 8 (over z, y), gy: 2 (over core).
Axes of the slice: x: 2, y: 2, z: 4, core: 2. Of those that a mesh axis runs over, the one named last changes fastest.
Arguments:
- currents: bfloat16 [64, 8, 2, 128, 256], P(('groups', 'gx'), 'gy'), parts along dimension 0, may hold values from -6 to 6
- self_blocks: bfloat16 [64, 8, 2, 256, 256], P(('groups', 'gx'), 'gy'), parts along dimension 0, may hold values from -0.25 to 0.25
- near_blocks: bfloat16 [16, 2, 40, 2, 256, 256], P(('groups', 'gx'), 'gy'), parts along dimension 0, may hold values from -0.25 to 0.25
- near_pairs: int32 [16, 2, 40, 2], P(('groups', 'gx'), 'gy'), parts along dimension 0, may hold values from 0 to 15, as said below
- near_count: int32 [16, 2], P(('groups', 'gx'), 'gy'), parts along dimension 0, may hold values from 1 to 40, as said below
- basis: bfloat16 [64, 8, 2, 32, 256], P(('groups', 'gx'), 'gy'), parts along dimension 0, may hold values from -0.375 to 0.375
- transfer: bfloat16 [64, 8, 2, 1024], P(('groups', 'gx'), 'gy'), parts along dimension 0, may hold values from -0.75 to 0.75
- coupling: bfloat16 [128, 64, 2, 1024], P(('groups', 'gx', 'gy')), parts along dimension 0, may hold values from -0.09375 to 0.09375
- far_shift: int32 [128, 64, 2], P(('groups', 'gx', 'gy')), parts along dimension 0, may hold values from -1 to 1
- far_mask: int32 [128, 64], P(('groups', 'gx', 'gy')), parts along dimension 0, may hold values 0 or 1
- parent: int32 [64, 8], P(('groups', 'gx'), 'gy'), parts along dimension 0, may hold values from 0 to 63, as said below
- bloch: float32 [4], P('groups'), parts along dimension 0, may hold values from -3.140625 to 3.140625
Outputs:
- product: bfloat16 [64, 8, 2, 128, 256], P(('groups', 'gx'), 'gy'), parts along dimension 0
The draws below stay inside these ranges and needn't reach their ends.
There are 2 independent parts, one for each index of `groups`. The reference program is written for one: setup_inputs(seed, part) draws one part's arguments, and reference() takes and returns one part's arrays. A program takes and returns all parts, laid end to end along the dimension named above; each array names one. Nothing has to cross between parts.
Inputs may be any that keep to these rules, and one draw needn't show every extreme that they name: `near_pairs`: column 0 is a block of the tile numbered i * 4 + j, column 1 a neighbour direction from 0 to 7; slots at or past the tile's live count hold entries of the same law. `near_count`: some tile holds exactly 40 live slots. A block of tile (tx, ty) has its parent among the 4 clusters from 4 * (tx * 2 + ty) on.
All inputs are finite; a program needn't handle non-finite values. No bound on the sum of `far_mask` on one device may be relied on, other than what follows from the above.
Results may differ from the reference program's by a relative error of at most 0.0042.
Values may be sent and summed in bfloat16 or wider, within the bound.
No kernel may reach another device: no remote copies, remote signals or barrier semaphores. Data moves between devices by JAX's collectives and lax.ppermute only.
A program may use at most 192 MiB of HBM per device.

```python
import jax
import jax.numpy as jnp
from jax import lax

P_SIZE = 256
K = 32
R = 128
BX_DEV = 4
BY_DEV = 4
CL_DEV = 4
PAIRS_DEV = 40
TILES_X = 8
TILES_Y = 2
NBX = 32
NBY = 8
NCL = 64
N_GX = 8
N_GY = 2


def draw_near_pairs(key, part):
    key = jax.random.fold_in(key, 11)
    key_rows, key_dirs, key_pick = jax.random.split(key, 3)
    tiles = TILES_X * TILES_Y
    row_part = jax.random.randint(key_rows, (tiles, PAIRS_DEV), 0, BX_DEV * BY_DEV)
    dir_part = jax.random.randint(key_dirs, (tiles, PAIRS_DEV), 0, 8)
    chosen = jax.random.randint(key_pick, (), 0, tiles)
    row_part = row_part.at[chosen, 0].set(BX_DEV * BY_DEV - 1)
    table = jnp.stack([row_part, dir_part], axis=-1)
    return table.reshape(TILES_X, TILES_Y, PAIRS_DEV, 2).astype(jnp.int32)


def draw_near_count(key, part):
    key = jax.random.fold_in(key, 12)
    key_count, key_pick = jax.random.split(key)
    tiles = TILES_X * TILES_Y
    counted = jax.random.randint(key_count, (tiles,), 1, PAIRS_DEV + 1)
    chosen = jax.random.randint(key_pick, (), 0, tiles)
    counted = counted.at[chosen].set(PAIRS_DEV)
    return counted.reshape(TILES_X, TILES_Y).astype(jnp.int32)


def draw_parent(key, part):
    key = jax.random.fold_in(key, 13)
    key_local, key_pos = jax.random.split(key)
    block_x = jnp.arange(NBX)[:, None]
    block_y = jnp.arange(NBY)[None, :]
    tile_x = block_x // BX_DEV
    tile_y = block_y // BY_DEV
    local = jax.random.randint(key_local, (NBX, NBY), 0, CL_DEV)
    marked = jax.random.randint(key_pos, (TILES_X, TILES_Y), 0, BX_DEV * BY_DEV)
    inside = block_x % BX_DEV * BY_DEV + block_y % BY_DEV
    local = jnp.where(inside == marked[tile_x, tile_y], CL_DEV - 1, local)
    return ((tile_x * TILES_Y + tile_y) * CL_DEV + local).astype(jnp.int32)


def set_ends(drawn, key, low, top_value):
    shape = drawn.shape
    index_at = [jax.random.randint(jax.random.fold_in(key, axis), (), 0, shape[axis]) for axis in range(len(shape))]
    drawn = drawn.at[tuple(index_at)].set(low)
    longest = shape.index(max(shape))
    index_at[longest] = (index_at[longest] + 1) % shape[longest]
    return drawn.at[tuple(index_at)].set(top_value)


def block_levels(rng, extent, cuts, least, top_value):
    level, own = 1.0, jax.random.fold_in(rng, 6)
    for axis_at, blocks in cuts:
        steps = jnp.exp(jax.random.uniform(jax.random.fold_in(own, axis_at), (blocks,), jnp.float32, least / len(cuts), top_value / len(cuts)))
        level = level * jnp.repeat(steps, extent[axis_at] // blocks).reshape([-1 if axis == axis_at else 1 for axis in range(len(extent))])
    return level


def normal_values(own_key, dims, scale, most, shards=(), held_as=jnp.bfloat16):
    level = block_levels(own_key, dims, shards, -0.22, 0.18) if shards else 1.0
    drawn = jax.random.normal(own_key, dims, jnp.float32) * scale * level
    return jnp.minimum(jnp.maximum(drawn, -most), most).astype(held_as)


def setup_inputs(seed: int = 0, part: int = 0) -> dict:
    splits = jax.random.split(jax.random.key(seed), 13)
    part_keys = jax.random.split(jax.random.fold_in(splits[12], part), 13)
    return {
        "currents": normal_values(part_keys[0], (NBX, NBY, 2, R, P_SIZE), 1.0, 6.0, ((0, 8), (1, 2))),
        "self_blocks": normal_values(part_keys[1], (NBX, NBY, 2, P_SIZE, P_SIZE), (2 * P_SIZE) ** -0.5, 0.25, ((0, 8), (1, 2))),
        "near_blocks": normal_values(part_keys[2], (TILES_X, TILES_Y, PAIRS_DEV, 2, P_SIZE, P_SIZE), (2 * P_SIZE) ** -0.5, 0.25, ((0, 8), (1, 2))),
        "near_pairs": draw_near_pairs(jax.random.fold_in(jax.random.fold_in(splits[12], part), 71), part),
        "near_count": draw_near_count(jax.random.fold_in(jax.random.fold_in(splits[12], part), 71), part),
        "basis": normal_values(part_keys[5], (NBX, NBY, 2, K, P_SIZE), P_SIZE ** -0.5, 0.375, ((0, 8), (1, 2))),
        "transfer": normal_values(part_keys[6], (NBX, NBY, 2, K * K), (2 * K) ** -0.5, 0.75, ((0, 8), (1, 2))),
        "coupling": normal_values(part_keys[7], (NCL, NCL, 2, K * K), (2 * K * NCL) ** -0.5, 0.09375, ((0, 16),)),
        "far_shift": set_ends(jax.random.randint(part_keys[8], (NCL, NCL, 2), -1, 2), jax.random.fold_in(part_keys[8], 1), -1, 1).astype(jnp.int32),
        "far_mask": set_ends((jax.random.randint(part_keys[9], (NCL, NCL), 0, 4) < 3).astype(jnp.int32), jax.random.fold_in(part_keys[9], 1), 0, 1),
        "parent": draw_parent(jax.random.fold_in(jax.random.fold_in(splits[12], part), 71), part),
        "bloch": jnp.clip(jax.random.uniform(part_keys[11], (2,), jnp.float32, -3.140625, 3.140625), -3.140625, 3.140625),
    }


HIGH = lax.Precision.HIGHEST


def cmul_block(mats, vals, form):
    real = jnp.einsum(form, mats[:, 0], vals[:, 0], precision=HIGH) - jnp.einsum(form, mats[:, 1], vals[:, 1], precision=HIGH)
    imag = jnp.einsum(form, mats[:, 0], vals[:, 1], precision=HIGH) + jnp.einsum(form, mats[:, 1], vals[:, 0], precision=HIGH)
    return jnp.stack([real, imag], axis=1)


def rounded(value):
    return lax.optimization_barrier(value.astype(jnp.bfloat16)).astype(jnp.float32)


def reference(currents, self_blocks, near_blocks, near_pairs, near_count, basis, transfer, coupling, far_shift, far_mask, parent, bloch):
    currents_f = currents.astype(jnp.float32)
    tiles = N_GX * N_GY
    mats_all = near_blocks.reshape(tiles, PAIRS_DEV, 2, P_SIZE, P_SIZE)
    pairs_all = near_pairs.reshape(tiles, PAIRS_DEV, 2)
    counts_all = near_count.reshape(tiles)

    def tile_term(running, scan_item):
        device_id, near_mats, pair_table, live_count = scan_item
        tile_x = device_id // N_GY
        tile_y = device_id % N_GY
        row_local = pair_table[:, 0]
        direction = pair_table[:, 1]
        offset = direction + (direction >= 4).astype(jnp.int32)
        row_x = tile_x * BX_DEV + row_local // BY_DEV
        row_y = tile_y * BY_DEV + row_local % BY_DEV
        pos_x = row_x + offset // 3 - 1
        pos_y = row_y + offset % 3 - 1
        shift_x = jnp.floor_divide(pos_x, NBX)
        shift_y = jnp.floor_divide(pos_y, NBY)
        col_x = pos_x - shift_x * NBX
        col_y = pos_y - shift_y * NBY
        phases = bloch[0] * shift_x.astype(jnp.float32) + bloch[1] * shift_y.astype(jnp.float32)
        phase_cos = jnp.cos(phases)[:, None, None]
        phase_sin = jnp.sin(phases)[:, None, None]
        alive_mask = (jnp.arange(PAIRS_DEV) < live_count).astype(jnp.float32)[:, None, None, None]
        sources = currents_f[col_x, col_y]
        row_vals = currents_f[row_x, row_y]
        column_source = rounded(jnp.stack([phase_cos * sources[:, 0] - phase_sin * sources[:, 1], phase_sin * sources[:, 0] + phase_cos * sources[:, 1]], axis=1))
        row_source = rounded(jnp.stack([phase_cos * row_vals[:, 0] + phase_sin * row_vals[:, 1], phase_cos * row_vals[:, 1] - phase_sin * row_vals[:, 0]], axis=1))
        mats_f = near_mats.astype(jnp.float32)
        forward = cmul_block(mats_f, column_source, "spq,sRq->sRp") * alive_mask
        transposed = cmul_block(mats_f, row_source, "spq,sRp->sRq") * alive_mask
        running = running.at[row_x, row_y].add(forward)
        running = running.at[col_x, col_y].add(transposed)
        return running, None

    near_field, _ = lax.scan(tile_term, jnp.zeros(currents.shape, jnp.float32), (jnp.arange(tiles, dtype=jnp.int32), mats_all, pairs_all, counts_all))

    blocks = NBX * NBY
    flat_cur = currents_f.reshape(blocks, 2, R, P_SIZE)
    self_field = cmul_block(self_blocks.astype(jnp.float32).reshape(blocks, 2, P_SIZE, P_SIZE), flat_cur, "spq,sRq->sRp")

    basis_f = basis.astype(jnp.float32).reshape(blocks, 2, K, P_SIZE)
    transfer_f = transfer.astype(jnp.float32).reshape(blocks, 2, K, K)
    leaf_coeff = cmul_block(basis_f, flat_cur, "skp,sRp->skR")
    lifted = cmul_block(transfer_f, leaf_coeff, "skl,slR->skR")
    cluster_coeff = rounded(jax.ops.segment_sum(lifted, parent.reshape(blocks), num_segments=NCL))

    def far_row(row_item):
        mats, shifts, keep = row_item
        mats = mats.astype(jnp.float32).reshape(NCL, 2, K, K)
        prod = cmul_block(mats, cluster_coeff, "qkl,qlR->qkR")
        phases = bloch[0] * shifts[:, 0].astype(jnp.float32) + bloch[1] * shifts[:, 1].astype(jnp.float32)
        weight_cos = (keep.astype(jnp.float32) * jnp.cos(phases))[:, None, None]
        weight_sin = (keep.astype(jnp.float32) * jnp.sin(phases))[:, None, None]
        real = jnp.sum(weight_cos * prod[:, 0] - weight_sin * prod[:, 1], axis=0)
        imag = jnp.sum(weight_sin * prod[:, 0] + weight_cos * prod[:, 1], axis=0)
        return jnp.stack([real, imag], axis=0)

    far_local = lax.map(far_row, (coupling, far_shift, far_mask))
    chosen = far_local[parent.reshape(blocks)]
    down_coeff = rounded(cmul_block(transfer_f, chosen, "skl,skR->slR"))
    far_field = cmul_block(basis_f, down_coeff, "skp,skR->sRp")
    total = near_field + (self_field + far_field).reshape(currents.shape)
    return total.astype(jnp.bfloat16)
```

```python
import functools

import jax
import jax.numpy as jnp
from jax import lax
from jax.experimental import pallas as pl
from jax.experimental.pallas import tpu as pltpu
from jax.sharding import PartitionSpec as P

F32 = jnp.float32
BF16 = jnp.bfloat16
RING = 6
VMEM_LIMIT = 48 * 1024 * 1024


def dot_nn(a, b):
    return lax.dot_general(a, b, (((1,), (0,)), ((), ())), preferred_element_type=F32)


def dot_nt(a, b):
    return lax.dot_general(a, b, (((1,), (1,)), ((), ())), preferred_element_type=F32)


def dot_tn(a, b):
    return lax.dot_general(a, b, (((0,), (0,)), ((), ())), preferred_element_type=F32)


def add_planes(acc, at, raw_r, raw_i, half, fresh=False):
    real = raw_r[:half] - raw_i[half:]
    imag = raw_r[half:] + raw_i[:half]
    if fresh:
        acc[at, :half, :] = real
        acc[at, half:, :] = imag
    else:
        acc[at, :half, :] += real
        acc[at, half:, :] += imag


def turned(value, cos, sin, half):
    re = value[:half].astype(F32)
    im = value[half:].astype(F32)
    return cos * re - sin * im, sin * re + cos * im


def slot_place(pairs, s, tile_y):
    r = pairs[2 * s]
    d = pairs[2 * s + 1]
    u = d + jnp.where(d >= 4, 1, 0)
    ux = jnp.where(u >= 6, 2, jnp.where(u >= 3, 1, 0))
    rx = lax.div(r, tile_y)
    ry = r - rx * tile_y
    return r, rx + ux, ry + u - 3 * ux


def pick_slots(pairs, count, chosen, tile_x, tile_y, crossing):
    def one(s, found):
        _, cx, _ = slot_place(pairs, s, tile_y)
        over = (cx == 0) | (cx == tile_x + 1)
        take = over if crossing else jnp.logical_not(over)

        @pl.when(take)
        def _():
            chosen[found] = s

        return found + jnp.where(take, 1, 0)

    return lax.fori_loop(0, count, one, 0)


def out_kernel(tile_x, tile_y, half, pairs, count, cos, sin, own, near, main, corner, chosen, acc, ring, sems):
    wide_y = tile_y + 2
    n = pick_slots(pairs, count[0], chosen, tile_x, tile_y, True)

    def copy(t):
        return pltpu.make_async_copy(near.at[chosen[t]], ring.at[lax.rem(t, RING)], sems.at[lax.rem(t, RING)])

    def start(t):
        @pl.when(t < n)
        def _():
            copy(t).start()

    for t in range(RING - 1):
        start(t)
    acc[...] = jnp.zeros_like(acc)

    def body(t, carry):
        copy(t).wait()
        start(t + RING - 1)
        mats = ring.at[lax.rem(t, RING)]
        r, cx, cy = slot_place(pairs, chosen[t], tile_y)
        x = own[r]
        at = jnp.where(cx == 0, 0, wide_y) + cy
        add_planes(acc, at, dot_nn(x, mats[0]), dot_nn(x, mats[1]), half)
        return carry

    lax.fori_loop(0, n, body, 0)
    for side in range(2):
        for cy in range(wide_y):
            w = (tile_x + 1) * side * wide_y + cy
            re, im = turned(acc.at[side * wide_y + cy], cos[w], -sin[w], half)
            if 0 < cy < wide_y - 1:
                main[side, cy - 1, :half, :] = re.astype(BF16)
                main[side, cy - 1, half:, :] = im.astype(BF16)
            else:
                corner[side, min(cy, 1), :half, :] = re.astype(BF16)
                corner[side, min(cy, 1), half:, :] = im.astype(BF16)


def fold_kernel(tile_y, main, corner, left, right):
    for side, out in ((0, left), (1, right)):
        for j in range(tile_y):
            total = main[side, j].astype(F32)
            if j == tile_y - 1:
                total = total + corner[side, 0].astype(F32)
            if j == 0:
                total = total + corner[side, 1].astype(F32)
            out[j] = total.astype(BF16)


def leaf_kernel(blocks, rank, half, parent, own, basis, moves, coeff, acc):
    acc[...] = jnp.zeros_like(acc)
    for b in range(blocks):
        raw = dot_nt(basis[b], own[b])
        real = raw[:rank, :half] - raw[rank:, half:]
        imag = raw[:rank, half:] + raw[rank:, :half]
        leaf = jnp.concatenate([real, imag], axis=0)
        high = leaf.astype(BF16)
        low = (leaf - high.astype(F32)).astype(BF16)
        acc[parent[b]] += dot_nn(moves[b], high) + dot_nn(moves[b], low)
    for q in range(acc.shape[0]):
        coeff[q * rank : (q + 1) * rank, :half] = acc[q, :rank].astype(BF16)
        coeff[q * rank : (q + 1) * rank, half:] = acc[q, rank:].astype(BF16)


def inner_kernel(
    tile_x, tile_y, half, pairs, count, cos, sin, own, beside, own_mats, near, total, back, chosen, win, acc, ring, sems, own_sem
):
    blocks = tile_x * tile_y
    wide_y = tile_y + 2
    fetch = pltpu.make_async_copy(own, win.at[pl.ds(0, blocks)], own_sem)
    fetch.start()
    n = pick_slots(pairs, count[0], chosen, tile_x, tile_y, False)

    def wait(t):
        pltpu.make_async_copy(near.at[0], ring.at[lax.rem(t, RING)], sems.at[lax.rem(t, RING)]).wait()

    def start(t):
        to, sem = ring.at[lax.rem(t, RING)], sems.at[lax.rem(t, RING)]

        @pl.when(t < blocks)
        def _():
            pltpu.make_async_copy(own_mats.at[t], to, sem).start()

        @pl.when((t >= blocks) & (t < blocks + n))
        def _():
            pltpu.make_async_copy(near.at[chosen[jnp.maximum(t - blocks, 0)]], to, sem).start()

    for t in range(RING - 1):
        start(t)
    acc[blocks:] = jnp.zeros((2 * tile_x,) + acc.shape[1:], F32)
    for side in range(2):
        for i in range(tile_x):
            w = (i + 1) * wide_y + side * (wide_y - 1)
            re, im = turned(beside.at[1 - side, i], cos[w], sin[w], half)
            win[blocks + side * tile_x + i, :half, :] = re.astype(BF16)
            win[blocks + side * tile_x + i, half:, :] = im.astype(BF16)
    fetch.wait()

    def own_body(t, carry):
        wait(t)
        start(t + RING - 1)
        mats = ring.at[lax.rem(t, RING)]
        x = win[t]
        add_planes(acc, t, dot_nt(x, mats[0]), dot_nt(x, mats[1]), half, True)
        return carry

    lax.fori_loop(0, blocks, own_body, 0)

    def near_body(t, carry):
        wait(t)
        start(t + RING - 1)
        mats = ring.at[lax.rem(t, RING)]
        r, cx, cy = slot_place(pairs, chosen[t - blocks], tile_y)
        inside = (cx - 1) * tile_y + cy - 1
        c = jnp.where(cy == 0, blocks + cx - 1, jnp.where(cy == wide_y - 1, blocks + tile_x + cx - 1, inside))
        x = win[c]
        add_planes(acc, r, dot_nt(x, mats[0]), dot_nt(x, mats[1]), half)
        x = win[r]
        add_planes(acc, c, dot_nn(x, mats[0]), dot_nn(x, mats[1]), half)
        return carry

    lax.fori_loop(blocks, blocks + n, near_body, 0)
    for side in range(2):
        for i in range(tile_x):
            w = (i + 1) * wide_y + side * (wide_y - 1)
            re, im = turned(acc.at[blocks + side * tile_x + i], cos[w], -sin[w], half)
            back[side, i, :half, :] = re.astype(BF16)
            back[side, i, half:, :] = im.astype(BF16)
    total[...] = acc[:blocks]


def far_kernel(
    tile_x, tile_y, half, rank, pieces, pairs, count, cos, sin, parent, place, near_total, back, coeff, other, coupling, moves,
    basis, from_left, from_right, corner, near, out, edge, chosen, win, acc, far, stage, ring, sems, out_sem
):
    blocks = tile_x * tile_y
    wide_y = tile_y + 2
    n = pick_slots(pairs, count[0], chosen, tile_x, tile_y, True)

    def copy(t):
        return pltpu.make_async_copy(near.at[chosen[t]], ring.at[lax.rem(t, RING)], sems.at[lax.rem(t, RING)])

    def start(t):
        @pl.when(t < n)
        def _():
            copy(t).start()

    for t in range(RING - 1):
        start(t)

    for side in range(2):
        for cy in range(wide_y):
            w = (tile_x + 1) * side * wide_y + cy
            if cy == 0:
                cell = corner.at[side, 1]
            elif cy == wide_y - 1:
                cell = corner.at[side, 0]
            else:
                cell = (from_left, from_right)[side].at[cy - 1]
            re, im = turned(cell, cos[w], sin[w], half)
            win[side * wide_y + cy, :half, :] = re.astype(BF16)
            win[side * wide_y + cy, half:, :] = im.astype(BF16)

    raw = jnp.zeros((acc.shape[1], 2 * half), F32)
    rows = coeff.shape[0] // pieces
    for source, mine in ((coeff, True), (other, False)):
        for k in range(pieces):
            tile = jnp.bitwise_xor(place[0], k) * 2 + (place[1] if mine else 1 - place[1])
            raw = raw + dot_nn(coupling[tile], source[k * rows : (k + 1) * rows, :])
    for p in range(far.shape[0]):
        top = raw[2 * rank * p : 2 * rank * p + rank]
        low = raw[2 * rank * p + rank : 2 * rank * (p + 1)]
        far[p, :rank, :] = top[:, :half] - low[:, half:]
        far[p, rank:, :] = -(top[:, half:] + low[:, :half])

    def block(b):
        chosen_far = far[parent[b]].astype(BF16)
        down = dot_tn(moves[b], chosen_far).astype(BF16)
        both = jnp.concatenate([down, jnp.concatenate([-down[rank:], down[:rank]], axis=0)], axis=1)
        value = dot_tn(both, basis[b]) + near_total[b]
        j = b % tile_y
        if j == tile_y - 1:
            value = value + back[0, b // tile_y].astype(F32)
        if j == 0:
            value = value + back[1, b // tile_y].astype(F32)
        return value

    inner = (tile_x - 2) * tile_y
    for b in range(tile_y, blocks - tile_y):
        stage[b - tile_y] = block(b).astype(BF16)
    put = pltpu.make_async_copy(stage, out.at[pl.ds(tile_y, inner)], out_sem)
    put.start()
    for j in range(tile_y):
        acc[j] = block(j)
        acc[tile_y + j] = block(blocks - tile_y + j)

    def body(t, carry):
        copy(t).wait()
        start(t + RING - 1)
        mats = ring.at[lax.rem(t, RING)]
        r, cx, cy = slot_place(pairs, chosen[t], tile_y)
        x = win[jnp.where(cx == 0, 0, wide_y) + cy]
        at = jnp.where(cx == 0, r, r - (tile_x - 2) * tile_y)
        add_planes(acc, at, dot_nt(x, mats[0]), dot_nt(x, mats[1]), half)
        return carry

    lax.fori_loop(0, n, body, 0)
    edge[...] = acc[...]
    put.wait()


def last_kernel(tile_x, tile_y, edge, to_first, to_last, unused, out, stage, sems):
    blocks = tile_x * tile_y
    del unused
    puts = []
    for side, came in ((0, to_first), (1, to_last)):
        for j in range(tile_y):
            stage[side, j] = (edge[side * tile_y + j] + came[j].astype(F32)).astype(BF16)
        put = pltpu.make_async_copy(stage.at[side], out.at[pl.ds(side * (blocks - tile_y), tile_y)], sems.at[side])
        put.start()
        puts.append(put)
    for put in puts:
        put.wait()


SMEM = pl.BlockSpec(memory_space=pltpu.SMEM)
VMEM = pl.BlockSpec(memory_space=pltpu.VMEM)
ANY = pl.BlockSpec(memory_space=pl.ANY)


def call(kernel, ins, in_specs, outs, out_specs, scratch, flops, moved, name, aliases=None):
    return pl.pallas_call(
        kernel,
        out_shape=outs,
        in_specs=in_specs,
        out_specs=out_specs,
        scratch_shapes=scratch,
        input_output_aliases=aliases or {},
        compiler_params=pltpu.CompilerParams(vmem_limit_bytes=VMEM_LIMIT),
        cost_estimate=pl.CostEstimate(flops=flops, bytes_accessed=moved, transcendentals=0),
        name=name,
    )(*ins)


def per_device(
    currents, self_blocks, near_blocks, near_pairs, near_count, basis, transfer, coupling, far_shift, far_mask, parent, bloch
):
    tile_x, tile_y, _, half, panels = currents.shape
    rank = basis.shape[3]
    blocks = tile_x * tile_y
    wide_x, wide_y = tile_x + 2, tile_y + 2
    gx_count, gy_count = lax.axis_size("gx"), lax.axis_size("gy")
    gx_index, gy_index = lax.axis_index("gx"), lax.axis_index("gy")
    clusters = far_mask.shape[0]
    tiles = gx_count * gy_count
    width = 2 * half
    slots = near_pairs.shape[2]

    def shape(*dims, dtype=BF16):
        return jax.ShapeDtypeStruct(dims, dtype)

    right = [(i, (i + 1) % gx_count) for i in range(gx_count)]
    left = [((i + 1) % gx_count, i) for i in range(gx_count)]
    swap = [(i, (i + 1) % gy_count) for i in range(gy_count)]

    own = currents.reshape(blocks, width, panels)
    from_left = lax.ppermute(own[blocks - tile_y :], "gx", right)
    from_right = lax.ppermute(own[:tile_y], "gx", left)
    columns = jnp.stack([currents[:, 0], currents[:, tile_y - 1]]).reshape(2, tile_x, width, panels)
    beside = lax.ppermute(columns, "gy", swap)

    pairs = near_pairs.reshape(2 * slots)
    count = near_count.reshape(1)
    near = near_blocks.reshape(slots, 2, panels, panels)
    own_mats = self_blocks.reshape(blocks, 2, panels, panels)
    steps_x = jnp.zeros((wide_x,), F32).at[0].set(jnp.where(gx_index == 0, -1.0, 0.0))
    steps_x = steps_x.at[wide_x - 1].set(jnp.where(gx_index == gx_count - 1, 1.0, 0.0))
    steps_y = jnp.zeros((wide_y,), F32).at[0].set(jnp.where(gy_index == 0, -1.0, 0.0))
    steps_y = steps_y.at[wide_y - 1].set(jnp.where(gy_index == gy_count - 1, 1.0, 0.0))
    phases = (bloch[0] * steps_x[:, None] + bloch[1] * steps_y[None, :]).reshape(-1)
    cos, sin = jnp.cos(phases), jnp.sin(phases)
    cluster_base = (gx_index * gy_count + gy_index) * clusters
    local_parent = parent.reshape(blocks) - cluster_base
    basis_b = basis.reshape(blocks, 2 * rank, panels)
    tr = transfer.reshape(blocks, 2, rank, rank)
    moves = jnp.concatenate(
        [jnp.concatenate([tr[:, 0], -tr[:, 1]], axis=2), jnp.concatenate([tr[:, 1], tr[:, 0]], axis=2)], axis=1
    )

    coeff = call(
        functools.partial(leaf_kernel, blocks, rank, half),
        (local_parent, own, basis_b, moves),
        [SMEM, VMEM, VMEM, VMEM],
        shape(clusters * rank, width),
        VMEM,
        [pltpu.VMEM((clusters, 2 * rank, half), F32)],
        2 * blocks * 2 * rank * panels * width,
        own.size * 2 + basis_b.size * 2,
        "leaf",
    )
    main, corner = call(
        functools.partial(out_kernel, tile_x, tile_y, half),
        (pairs, count, cos, sin, own, near),
        [SMEM, SMEM, SMEM, SMEM, VMEM, ANY],
        [shape(2, tile_y, width, panels), shape(2, 2, width, panels)],
        [VMEM, VMEM],
        [
            pltpu.SMEM((slots,), jnp.int32),
            pltpu.VMEM((2 * wide_y, width, panels), F32),
            pltpu.VMEM((RING, 2, panels, panels), BF16),
            pltpu.SemaphoreType.DMA((RING,)),
        ],
        2 * 10 * 2 * width * panels * panels,
        own.size * 2 + 10 * 2 * 2 * panels * panels,
        "outward",
    )
    corner_in = lax.ppermute(corner, "gy", swap)
    back_left, back_right = call(
        functools.partial(fold_kernel, tile_y),
        (main, corner_in),
        [VMEM, VMEM],
        [shape(tile_y, width, panels), shape(tile_y, width, panels)],
        [VMEM, VMEM],
        [],
        main.size,
        main.size * 6,
        "fold",
    )
    to_last = lax.ppermute(back_left, "gx", left)
    to_first = lax.ppermute(back_right, "gx", right)

    bit = 1
    while bit < gx_count:
        other = lax.ppermute(coeff, "gx", [(i, i ^ bit) for i in range(gx_count)])
        coeff = jnp.concatenate([coeff, other], axis=0)
        bit *= 2
    other = lax.ppermute(coeff, "gy", swap)

    near_total, y_back = call(
        functools.partial(inner_kernel, tile_x, tile_y, half),
        (pairs, count, cos, sin, own, beside, own_mats, near),
        [SMEM, SMEM, SMEM, SMEM, ANY, VMEM, ANY, ANY],
        [shape(blocks, width, panels, dtype=F32), shape(2, tile_x, width, panels)],
        [VMEM, VMEM],
        [
            pltpu.SMEM((slots,), jnp.int32),
            pltpu.VMEM((blocks + 2 * tile_x, width, panels), BF16),
            pltpu.VMEM((blocks + 2 * tile_x, width, panels), F32),
            pltpu.VMEM((RING, 2, panels, panels), BF16),
            pltpu.SemaphoreType.DMA((RING,)),
            pltpu.SemaphoreType.DMA,
        ],
        2 * (2 * slots * 3 // 4 + blocks) * 2 * width * panels * panels,
        near.size * 2 + own_mats.size * 2 + own.size * 8,
        "inner",
    )
    back = lax.ppermute(y_back, "gy", swap)

    pair_phase = bloch[0] * far_shift[..., 0].astype(F32) + bloch[1] * far_shift[..., 1].astype(F32)
    keep = far_mask.astype(F32)
    weight_cos = (keep * jnp.cos(pair_phase)).reshape(clusters, tiles, clusters, 1, 1)
    weight_sin = (keep * jnp.sin(pair_phase)).reshape(clusters, tiles, clusters, 1, 1)
    mats = coupling.reshape(clusters, tiles, clusters, 2, rank, rank).astype(F32)
    mats = jnp.stack(
        [
            weight_cos * mats[:, :, :, 0] - weight_sin * mats[:, :, :, 1],
            weight_sin * mats[:, :, :, 0] + weight_cos * mats[:, :, :, 1],
        ],
        axis=3,
    ).astype(BF16)
    mats = mats.transpose(1, 0, 3, 4, 2, 5).reshape(tiles, clusters * 2 * rank, clusters * rank)

    halo_corner = jnp.stack(
        [from_left[0], from_left[tile_y - 1], from_right[0], from_right[tile_y - 1]]
    ).reshape(2, 2, width, panels)
    halo_corner = lax.ppermute(halo_corner, "gy", swap)
    place = jnp.stack([gx_index, gy_index]).astype(jnp.int32)
    out, edge = call(
        functools.partial(far_kernel, tile_x, tile_y, half, rank, gx_count),
        (
            pairs, count, cos, sin, local_parent, place, near_total, back, coeff, other, mats, moves, basis_b, from_left,
            from_right, halo_corner, near,
        ),
        [SMEM] * 6 + [VMEM] * 10 + [ANY],
        [shape(blocks, width, panels), shape(2 * tile_y, width, panels, dtype=F32)],
        [ANY, VMEM],
        [
            pltpu.SMEM((slots,), jnp.int32),
            pltpu.VMEM((2 * wide_y, width, panels), BF16),
            pltpu.VMEM((2 * tile_y, width, panels), F32),
            pltpu.VMEM((clusters, 2 * rank, half), F32),
            pltpu.VMEM(((tile_x - 2) * tile_y, width, panels), BF16),
            pltpu.VMEM((RING, 2, panels, panels), BF16),
            pltpu.SemaphoreType.DMA((RING,)),
            pltpu.SemaphoreType.DMA,
        ],
        2 * 20 * 2 * width * panels * panels,
        near_total.size * 4 + coupling.size * 2 + own.size * 4 + 10 * 2 * 2 * panels * panels,
        "far",
    )
    out = call(
        functools.partial(last_kernel, tile_x, tile_y),
        (edge, to_first, to_last, out),
        [VMEM, VMEM, VMEM, ANY],
        shape(blocks, width, panels),
        ANY,
        [pltpu.VMEM((2, tile_y, width, panels), BF16), pltpu.SemaphoreType.DMA((2,))],
        edge.size,
        edge.size * 8,
        "last",
        aliases={3: 0},
    )
    return out.reshape(currents.shape)


def solution(mesh):
    placed = (
        P(("groups", "gx"), "gy", None, None, None),
        P(("groups", "gx"), "gy", None, None, None),
        P(("groups", "gx"), "gy", None, None, None, None),
        P(("groups", "gx"), "gy", None, None),
        P(("groups", "gx"), "gy"),
        P(("groups", "gx"), "gy", None, None, None),
        P(("groups", "gx"), "gy", None, None),
        P(("groups", "gx", "gy"), None, None, None),
        P(("groups", "gx", "gy"), None, None),
        P(("groups", "gx", "gy"), None),
        P(("groups", "gx"), "gy"),
        P("groups"),
    )
    return jax.shard_map(
        per_device,
        mesh=mesh,
        in_specs=placed,
        out_specs=P(("groups", "gx"), "gy", None, None, None),
        check_vma=False,
    )
```

```python
import functools

import jax
import jax.numpy as jnp
from jax import lax
from jax.experimental import pallas as pl
from jax.experimental.pallas import tpu as pltpu
from jax.sharding import PartitionSpec as P

F32 = jnp.float32
BF16 = jnp.bfloat16
GROUP = 4
DEPTH = 3
VMEM_LIMIT = 48 * 1024 * 1024


def dot_nn(a, b):
    return lax.dot_general(a, b, (((1,), (0,)), ((), ())), preferred_element_type=F32)


def dot_nt(a, b):
    return lax.dot_general(a, b, (((1,), (1,)), ((), ())), preferred_element_type=F32)


def dot_tn(a, b):
    return lax.dot_general(a, b, (((0,), (0,)), ((), ())), preferred_element_type=F32)


def set_pair(win, at, re, im, half):
    panels = re.shape[1]
    win[at, :half, :panels] = re
    win[at, half:, :panels] = im
    win[at, :half, panels:] = -im
    win[at, half:, panels:] = re


def forward(pair, mats):
    return dot_nt(pair, jnp.concatenate([mats[0], mats[1]], axis=1))


def transposed(pair, mats):
    return dot_nn(pair, jnp.concatenate([mats[0], mats[1]], axis=0))


def turned(value, cos, sin, half):
    re = value[:half].astype(F32)
    im = value[half:].astype(F32)
    return cos * re - sin * im, sin * re + cos * im


def cell_phase(bloch, x, y, wide_x, wide_y, panels):
    shift_x = shift_y = 0.0
    if x == 0:
        shift_x = jnp.where(lax.axis_index("gx") == 0, -1.0, 0.0)
    if x == wide_x - 1:
        shift_x = jnp.where(lax.axis_index("gx") == lax.axis_size("gx") - 1, 1.0, 0.0)
    if y == 0:
        shift_y = jnp.where(lax.axis_index("gy") == 0, -1.0, 0.0)
    if y == wide_y - 1:
        shift_y = jnp.where(lax.axis_index("gy") == lax.axis_size("gy") - 1, 1.0, 0.0)
    phase = jnp.full((1, panels), bloch[0] * shift_x + bloch[1] * shift_y, F32)
    return jnp.cos(phase), jnp.sin(phase)


def slot_place(pairs, s, tile_y):
    r = pairs[0, s]
    d = pairs[1, s]
    u = d + jnp.where(d >= 4, 1, 0)
    ux = jnp.where(u >= 6, 2, jnp.where(u >= 3, 1, 0))
    rx = lax.div(r, tile_y)
    ry = r - rx * tile_y
    return r, rx + ux, ry + u - 3 * ux


def pick_slots(pairs, count, chosen, tile_x, tile_y, wanted):
    for s in range(chosen.shape[0]):
        chosen[s] = 0

    def one(s, found):
        _, cx, cy = slot_place(pairs, s, tile_y)
        take = wanted(cx, cy)

        @pl.when(take)
        def _():
            chosen[found] = s

        return found + jnp.where(take, 1, 0)

    n = lax.fori_loop(0, count, one, 0)
    return n, lax.div(n + GROUP - 1, GROUP)


def stream(groups, fetch, ring, sems, body):
    def start(g):
        @pl.when(g < groups)
        def _():
            at = lax.rem(g, DEPTH)
            for k in range(GROUP):
                fetch(g * GROUP + k, ring.at[at, k], sems.at[at, k])

    def prime():
        for g in range(DEPTH - 1):
            start(g)

    def step(g, carry):
        at = lax.rem(g, DEPTH)
        for k in range(GROUP):
            pltpu.make_async_copy(ring.at[at, k], ring.at[at, k], sems.at[at, k]).wait()
        start(g + DEPTH - 1)
        body(g, at)
        return carry

    return prime, lambda first, last: lax.fori_loop(first, last, step, 0)


def out_kernel(
    tile_x, tile_y, half, pairs, count, bloch, own, near, main, low_corner, high_corner, beside, chosen, win, acc, ring, sems
):
    blocks = tile_x * tile_y
    wide_x, wide_y = tile_x + 2, tile_y + 2
    panels = own.shape[2]

    def outside(cx, cy):
        return (cx == 0) | (cx == wide_x - 1) | (cy == 0) | (cy == wide_y - 1)

    n, groups = pick_slots(pairs, count[0, 0], chosen, tile_x, tile_y, outside)

    def fetch(t, to, sem):
        pltpu.make_async_copy(near.at[chosen[t]], to, sem).start()

    def body(g, at):
        for k in range(GROUP):
            t = g * GROUP + k
            r, cx, cy = slot_place(pairs, chosen[t], tile_y)
            over = jnp.where(cx == 0, 0, wide_y) + cy
            along = 2 * wide_y + jnp.where(cy == 0, 0, tile_x) + cx - 1
            c = jnp.where((cx == 0) | (cx == wide_x - 1), over, along)
            acc[jnp.where(t < n, c, 2 * wide_y + 2 * tile_x)] += transposed(win[r], ring[at, k])

    prime, run = stream(groups, fetch, ring, sems, body)
    prime()
    for b in range(blocks):
        set_pair(win, b, own[b, :half], own[b, half:], half)
    acc[...] = jnp.zeros_like(acc)
    run(0, groups)
    for side in range(2):
        for cy in range(wide_y):
            cos, sin = cell_phase(bloch, (wide_x - 1) * side, cy, wide_x, wide_y, panels)
            re, im = turned(acc.at[side * wide_y + cy], cos, -sin, half)
            if 0 < cy < wide_y - 1:
                main[side, cy - 1, :half, :] = re.astype(BF16)
                main[side, cy - 1, half:, :] = im.astype(BF16)
            else:
                corner = (low_corner, high_corner)[side]
                corner[min(cy, 1), :half, :] = re.astype(BF16)
                corner[min(cy, 1), half:, :] = im.astype(BF16)
        for i in range(tile_x):
            cos, sin = cell_phase(bloch, i + 1, (wide_y - 1) * side, wide_x, wide_y, panels)
            re, im = turned(acc.at[2 * wide_y + side * tile_x + i], cos, -sin, half)
            beside[side, i, :half, :] = re.astype(BF16)
            beside[side, i, half:, :] = im.astype(BF16)


def fold_kernel(tile_y, main, low_corner, high_corner, left, right):
    for side, corner, out in ((0, low_corner, left), (1, high_corner, right)):
        for j in range(tile_y):
            total = main[side, j].astype(F32)
            if j == tile_y - 1:
                total = total + corner[0].astype(F32)
            if j == 0:
                total = total + corner[1].astype(F32)
            out[j] = total.astype(BF16)


def edge_kernel(tile_x, tile_y, own, first, last, columns, sems):
    blocks = tile_x * tile_y
    puts = [
        pltpu.make_async_copy(own.at[pl.ds(0, tile_y)], first, sems.at[0]),
        pltpu.make_async_copy(own.at[pl.ds(blocks - tile_y, tile_y)], last, sems.at[1]),
    ]
    for i in range(tile_x):
        for side in range(2):
            cell = own.at[i * tile_y + side * (tile_y - 1)]
            puts.append(pltpu.make_async_copy(cell, columns.at[side, i], sems.at[2 + 2 * i + side]))
    for put in puts:
        put.start()
    for put in puts:
        put.wait()


def turn_kernel(rank, mats, out, flat):
    lanes = flat.shape[1]
    for p in range(mats.shape[0]):
        for at in range(0, mats.shape[1], lanes):
            flat[...] = mats[p, at : at + lanes].T
            for l in range(rank):
                rows = flat[pl.ds(l, rank, stride=rank), :]
                out[l, p * rank : (p + 1) * rank, at : at + lanes] = rows.astype(BF16)


def leaf_kernel(blocks, rank, half, parent, own, basis, moves, unused, coeff, acc):
    del unused
    base = (lax.axis_index("gx") * lax.axis_size("gy") + lax.axis_index("gy")) * acc.shape[0]
    acc[...] = jnp.zeros_like(acc)
    for b in range(blocks):
        raw = dot_nt(basis[b], own[b])
        real = raw[:rank, :half] - raw[rank:, half:]
        imag = raw[:rank, half:] + raw[rank:, :half]
        leaf = jnp.concatenate([real, imag], axis=0)
        high = leaf.astype(BF16)
        low = (leaf - high.astype(F32)).astype(BF16)
        acc[parent[b // parent.shape[1], b % parent.shape[1]] - base] += dot_nn(moves[b], high) + dot_nn(moves[b], low)
    for q in range(acc.shape[0]):
        coeff[q * rank : (q + 1) * rank, :half] = acc[q, :rank].astype(BF16)
        coeff[q * rank : (q + 1) * rank, half:] = acc[q, rank:].astype(BF16)


def self_kernel(blocks, half, own, own_mats, total, win, ring, sems):
    groups = blocks // GROUP

    def fetch(t, to, sem):
        pltpu.make_async_copy(own_mats.at[t], to, sem).start()

    def body(g, at):
        for k in range(GROUP):
            t = g * GROUP + k
            set_pair(win, k, own[t, :half], own[t, half:], half)
        for k in range(GROUP):
            total[g * GROUP + k] = forward(win[k], ring[at, k])

    prime, run = stream(groups, fetch, ring, sems, body)
    prime()
    run(0, groups)


def inner_kernel(
    tile_x, tile_y, half, pairs, count, bloch, own, beside, self_total, near, unused, total, chosen, win, acc, ring, sems, own_sem
):
    del unused
    blocks = tile_x * tile_y
    wide_x, wide_y = tile_x + 2, tile_y + 2
    panels = own.shape[2]
    begin = pltpu.make_async_copy(self_total, acc.at[pl.ds(0, blocks)], own_sem)
    n, groups = pick_slots(
        pairs, count[0, 0], chosen, tile_x, tile_y, lambda cx, cy: (cx > 0) & (cx < wide_x - 1)
    )

    def fetch(t, to, sem):
        pltpu.make_async_copy(near.at[chosen[t]], to, sem).start()

    def body(g, at):
        for k in range(GROUP):
            t = g * GROUP + k
            r, cx, cy = slot_place(pairs, chosen[t], tile_y)
            inside = (cx - 1) * tile_y + cy - 1
            out = (cy == 0) | (cy == wide_y - 1)
            c = jnp.where(out, blocks + jnp.where(cy == 0, 0, tile_x) + cx - 1, inside)
            acc[jnp.where(t < n, r, blocks)] += forward(win[jnp.where(t < n, c, 0)], ring[at, k])
            acc[jnp.where((t < n) & jnp.logical_not(out), inside, blocks)] += transposed(win[r], ring[at, k])

    prime, run = stream(groups, fetch, ring, sems, body)
    prime()
    begin.start()
    for b in range(blocks):
        set_pair(win, b, own[b, :half], own[b, half:], half)
    for side in range(2):
        for i in range(tile_x):
            cos, sin = cell_phase(bloch, i + 1, side * (wide_y - 1), wide_x, wide_y, panels)
            re, im = turned(beside.at[1 - side, i], cos, sin, half)
            set_pair(win, blocks + side * tile_x + i, re.astype(BF16), im.astype(BF16), half)
    begin.wait()
    run(0, groups)
    total[...] = acc[:blocks]


def far_kernel(
    tile_x, tile_y, half, rank, pieces, pairs, count, bloch, parent, near_total, back, coeff, other, coupling, moves,
    basis, from_left, from_right, corner, near, out, edge, chosen, win, acc, far, gathered, stage, ring, sems, out_sem
):
    blocks = tile_x * tile_y
    wide_x, wide_y = tile_x + 2, tile_y + 2
    panels = basis.shape[2]
    gx_index, gy_index = lax.axis_index("gx"), lax.axis_index("gy")
    base = (gx_index * lax.axis_size("gy") + gy_index) * far.shape[0]
    n, groups = pick_slots(
        pairs, count[0, 0], chosen, tile_x, tile_y, lambda cx, cy: (cx == 0) | (cx == wide_x - 1)
    )

    def fetch(t, to, sem):
        pltpu.make_async_copy(near.at[chosen[t]], to, sem).start()

    def body(g, at):
        for k in range(GROUP):
            t = g * GROUP + k
            r, cx, cy = slot_place(pairs, chosen[t], tile_y)
            x = win[jnp.where(t < n, jnp.where(cx == 0, 0, wide_y) + cy, 0)]
            row = jnp.where(cx == 0, r, r - (tile_x - 2) * tile_y)
            acc[jnp.where(t < n, row, 2 * tile_y)] += forward(x, ring[at, k])

    prime, run = stream(groups, fetch, ring, sems, body)
    prime()
    for side in range(2):
        for cy in range(wide_y):
            if cy == 0:
                cell = corner.at[side, 1]
            elif cy == wide_y - 1:
                cell = corner.at[side, 0]
            else:
                cell = (from_left, from_right)[side].at[cy - 1]
            cos, sin = cell_phase(bloch, (wide_x - 1) * side, cy, wide_x, wide_y, panels)
            re, im = turned(cell, cos, sin, half)
            set_pair(win, side * wide_y + cy, re.astype(BF16), im.astype(BF16), half)

    rows = coeff.shape[0] // pieces
    for source, core in ((coeff, gy_index), (other, 1 - gy_index)):
        for k in range(pieces):
            tile = jnp.bitwise_xor((k // 2) * 2 + jnp.bitwise_and(gx_index, 1), k % 2) * 2 + core
            at = pl.multiple_of(tile * rows, rows)
            for plane in range(2):
                piece = source[k * rows : (k + 1) * rows, plane * half : (plane + 1) * half]
                gathered[plane, pl.ds(at, rows), :] = piece.astype(F32)
    every = gathered.shape[1] // rank
    reals, imags = gathered.at[0], gathered.at[1]
    raw = jnp.zeros((coupling.shape[1], 2 * half), F32)
    for l in range(0, rank, 2):
        terms = []
        for m in (l, l + 1):
            re = reals[pl.ds(m, every, stride=rank), :]
            im = imags[pl.ds(m, every, stride=rank), :]
            terms.append(jnp.concatenate([re, im], axis=1).astype(BF16))
            terms.append(jnp.concatenate([-im, re], axis=1).astype(BF16))
        raw = raw + dot_nn(jnp.concatenate([coupling[l], coupling[l + 1]], axis=1), jnp.concatenate(terms, axis=0))
    for p in range(far.shape[0]):
        far[p, :rank, :] = raw[rank * p : rank * (p + 1), :half]
        far[p, rank:, :] = -raw[rank * p : rank * (p + 1), half:]

    def block(b):
        chosen_far = far[parent[b // tile_y, b % tile_y] - base]
        high = chosen_far.astype(BF16)
        low = (chosen_far - high.astype(F32)).astype(BF16)
        down = (dot_tn(moves[b], high) + dot_tn(moves[b], low)).astype(BF16)
        both = jnp.concatenate([down, jnp.concatenate([-down[rank:], down[:rank]], axis=0)], axis=1)
        value = dot_tn(both, basis[b]) + near_total[b]
        j = b % tile_y
        if j == tile_y - 1:
            value = value + back[0, b // tile_y].astype(F32)
        if j == 0:
            value = value + back[1, b // tile_y].astype(F32)
        return value

    inner = (tile_x - 2) * tile_y
    for b in range(tile_y, blocks - tile_y):
        stage[b - tile_y] = block(b).astype(BF16)
    put = pltpu.make_async_copy(stage, out.at[pl.ds(tile_y, inner)], out_sem)
    put.start()
    for j in range(tile_y):
        acc[j] = block(j)
        acc[tile_y + j] = block(blocks - tile_y + j)

    run(0, groups)
    edge[...] = acc[: 2 * tile_y]
    put.wait()


def last_kernel(tile_x, tile_y, edge, to_first, to_last, unused, out, whole, came, stage, sems):
    del unused
    blocks = tile_x * tile_y
    steps = []
    for side, source in ((0, to_first), (1, to_last)):
        for j in range(tile_y):
            c = side * tile_y + j
            to = j + side * (blocks - tile_y)
            steps.append(
                (
                    pltpu.make_async_copy(source.at[j], came.at[c], sems.at[0, c]),
                    pltpu.make_async_copy(edge.at[c], whole.at[c], sems.at[1, c]),
                    pltpu.make_async_copy(stage.at[c], out.at[to], sems.at[2, c]),
                )
            )
    for one, two, _ in steps:
        one.start()
        two.start()
    for c, (one, two, put) in enumerate(steps):
        one.wait()
        two.wait()
        stage[c] = (whole[c] + came[c].astype(F32)).astype(BF16)
        put.start()
    for _, _, put in steps:
        put.wait()


SMEM = pl.BlockSpec(memory_space=pltpu.SMEM)
VMEM = pl.BlockSpec(memory_space=pltpu.VMEM)
ANY = pl.BlockSpec(memory_space=pl.ANY)


def call(kernel, ins, in_specs, outs, out_specs, scratch, flops, moved, name, aliases=None):
    return pl.pallas_call(
        kernel,
        out_shape=outs,
        in_specs=in_specs,
        out_specs=out_specs,
        scratch_shapes=scratch,
        input_output_aliases=aliases or {},
        compiler_params=pltpu.CompilerParams(vmem_limit_bytes=VMEM_LIMIT),
        cost_estimate=pl.CostEstimate(flops=flops // 100, bytes_accessed=moved // 100, transcendentals=0),
        name=name,
    )(*ins)


def per_device(
    currents, self_blocks, near_blocks, near_pairs, near_count, basis, transfer, coupling, far_shift, far_mask, parent, bloch
):
    tile_x, tile_y, _, half, panels = currents.shape
    rank = basis.shape[3]
    blocks = tile_x * tile_y
    wide_x, wide_y = tile_x + 2, tile_y + 2
    gx_count, gy_count = lax.axis_size("gx"), lax.axis_size("gy")
    gx_index, gy_index = lax.axis_index("gx"), lax.axis_index("gy")
    clusters = far_mask.shape[0]
    tiles = gx_count * gy_count
    width = 2 * half
    slots = near_pairs.shape[2]

    def shape(*dims, dtype=BF16):
        return jax.ShapeDtypeStruct(dims, dtype)

    right = [(i, (i + 1) % gx_count) for i in range(gx_count)]
    left = [((i + 1) % gx_count, i) for i in range(gx_count)]
    swap = [(i, (i + 1) % gy_count) for i in range(gy_count)]

    own = currents.reshape(blocks, width, panels)
    first, last, columns = call(
        functools.partial(edge_kernel, tile_x, tile_y),
        (own,),
        [ANY],
        [shape(tile_y, width, panels), shape(tile_y, width, panels), shape(2, tile_x, width, panels)],
        [ANY, ANY, ANY],
        [pltpu.SemaphoreType.DMA((2 + 2 * tile_x,))],
        own.size,
        own.size * 4,
        "edges",
    )
    from_left = lax.ppermute(last, "gx", right)
    from_right = lax.ppermute(first, "gx", left)
    beside = lax.ppermute(columns, "gy", swap)

    pairs = near_pairs.reshape(slots, 2).T
    count = near_count
    near = near_blocks.reshape(slots, 2, panels, panels)
    own_mats = self_blocks.reshape(blocks, 2, panels, panels)
    basis_b = basis.reshape(blocks, 2 * rank, panels)
    tr = transfer.reshape(blocks, 2, rank, rank)
    moves = jnp.concatenate(
        [jnp.concatenate([tr[:, 0], -tr[:, 1]], axis=2), jnp.concatenate([tr[:, 1], tr[:, 0]], axis=2)], axis=1
    )

    main, low_corner, high_corner, beside_out = call(
        functools.partial(out_kernel, tile_x, tile_y, half),
        (pairs, count, bloch, own, near),
        [SMEM, SMEM, SMEM, VMEM, ANY],
        [shape(2, tile_y, width, panels), shape(2, width, panels), shape(2, width, panels), shape(2, tile_x, width, panels)],
        [VMEM] * 4,
        [
            pltpu.SMEM((slots + GROUP,), jnp.int32),
            pltpu.VMEM((blocks, width, 2 * panels), BF16),
            pltpu.VMEM((2 * wide_y + 2 * tile_x + 1, width, panels), F32),
            pltpu.VMEM((DEPTH, GROUP, 2, panels, panels), BF16),
            pltpu.SemaphoreType.DMA((DEPTH, GROUP)),
        ],
        2 * 10 * 2 * width * panels * panels,
        own.size * 2 + 10 * 2 * 2 * panels * panels,
        "outward",
    )
    low_corner = lax.ppermute(low_corner, "gy", swap)
    high_corner = lax.ppermute(high_corner, "gy", swap)
    back = lax.ppermute(beside_out, "gy", swap)
    coeff = call(
        functools.partial(leaf_kernel, blocks, rank, half),
        (parent, own, basis_b, moves, first),
        [SMEM, VMEM, VMEM, VMEM, ANY],
        shape(clusters * rank, width),
        VMEM,
        [pltpu.VMEM((clusters, 2 * rank, half), F32)],
        2 * blocks * 2 * rank * panels * width,
        own.size * 2 + basis_b.size * 2,
        "leaf",
    )
    back_left, back_right = call(
        functools.partial(fold_kernel, tile_y),
        (main, low_corner, high_corner),
        [VMEM, VMEM, VMEM],
        [shape(tile_y, width, panels), shape(tile_y, width, panels)],
        [VMEM, VMEM],
        [],
        main.size,
        main.size * 6,
        "fold",
    )
    from_left, from_right, back_left, back_right = lax.optimization_barrier((from_left, from_right, back_left, back_right))
    to_last = lax.ppermute(back_left, "gx", left)
    to_first = lax.ppermute(back_right, "gx", right)

    self_total = call(
        functools.partial(self_kernel, blocks, half),
        (own, own_mats),
        [VMEM, ANY],
        shape(blocks, width, panels, dtype=F32),
        VMEM,
        [
            pltpu.VMEM((GROUP, width, 2 * panels), BF16),
            pltpu.VMEM((DEPTH, GROUP, 2, panels, panels), BF16),
            pltpu.SemaphoreType.DMA((DEPTH, GROUP)),
        ],
        0,
        0,
        "itself",
    )
    other = lax.ppermute(coeff, "gx", [(i, i ^ 1) for i in range(gx_count)])
    coeff = jnp.concatenate([coeff, other], axis=0)
    coeff = lax.all_to_all(
        jnp.broadcast_to(coeff[None], (gx_count // 2,) + coeff.shape),
        "gx",
        0,
        0,
        axis_index_groups=[list(range(k, gx_count, 2)) for k in range(2)],
    ).reshape(-1, width)
    coeff, self_total = lax.optimization_barrier((coeff, self_total))
    other = lax.ppermute(coeff, "gy", swap)

    near_total = call(
        functools.partial(inner_kernel, tile_x, tile_y, half),
        (pairs, count, bloch, own, beside, self_total, near, from_left),
        [SMEM, SMEM, SMEM, VMEM, VMEM, ANY, ANY, ANY],
        shape(blocks, width, panels, dtype=F32),
        VMEM,
        [
            pltpu.SMEM((slots + GROUP,), jnp.int32),
            pltpu.VMEM((blocks + 2 * tile_x, width, 2 * panels), BF16),
            pltpu.VMEM((blocks + 1, width, panels), F32),
            pltpu.VMEM((DEPTH, GROUP, 2, panels, panels), BF16),
            pltpu.SemaphoreType.DMA((DEPTH, GROUP)),
            pltpu.SemaphoreType.DMA,
        ],
        0,
        0,
        "inner",
    )
    pair_phase = bloch[0] * far_shift[..., 0].astype(F32) + bloch[1] * far_shift[..., 1].astype(F32)
    keep = far_mask.astype(F32)
    weight_cos = (keep * jnp.cos(pair_phase))[:, :, None]
    weight_sin = (keep * jnp.sin(pair_phase))[:, :, None]
    mats = coupling.astype(F32)
    mats = jnp.concatenate(
        [
            weight_cos * mats[:, :, 0] - weight_sin * mats[:, :, 1],
            weight_sin * mats[:, :, 0] + weight_cos * mats[:, :, 1],
        ],
        axis=1,
    )
    sources = mats.shape[1]
    mats = call(
        functools.partial(turn_kernel, rank),
        (mats,),
        [VMEM],
        shape(rank, clusters * rank, sources),
        VMEM,
        [pltpu.VMEM((rank * rank, min(sources, 128)), F32)],
        coupling.size,
        coupling.size * 6,
        "turn",
    )

    halo_corner = jnp.stack(
        [from_left[0], from_left[tile_y - 1], from_right[0], from_right[tile_y - 1]]
    ).reshape(2, 2, width, panels)
    halo_corner = lax.ppermute(halo_corner, "gy", swap)
    out, edge = call(
        functools.partial(far_kernel, tile_x, tile_y, half, rank, gx_count),
        (
            pairs, count, bloch, parent, near_total, back, coeff, other, mats, moves, basis_b, from_left, from_right,
            halo_corner, near,
        ),
        [SMEM] * 4 + [VMEM] * 10 + [ANY],
        [shape(blocks, width, panels), shape(2 * tile_y, width, panels, dtype=F32)],
        [ANY, VMEM],
        [
            pltpu.SMEM((slots + GROUP,), jnp.int32),
            pltpu.VMEM((2 * wide_y, width, 2 * panels), BF16),
            pltpu.VMEM((2 * tile_y + 1, width, panels), F32),
            pltpu.VMEM((clusters, 2 * rank, half), F32),
            pltpu.VMEM((2, clusters * tiles * rank, half), F32),
            pltpu.VMEM(((tile_x - 2) * tile_y, width, panels), BF16),
            pltpu.VMEM((DEPTH, GROUP, 2, panels, panels), BF16),
            pltpu.SemaphoreType.DMA((DEPTH, GROUP)),
            pltpu.SemaphoreType.DMA,
        ],
        2 * 20 * 2 * width * panels * panels,
        near_total.size * 4 + coupling.size * 2 + own.size * 4 + 10 * 2 * 2 * panels * panels,
        "far",
    )
    cells = (2 * tile_y, width, panels)
    out = call(
        functools.partial(last_kernel, tile_x, tile_y),
        (edge, to_first, to_last, out),
        [ANY, ANY, ANY, ANY],
        shape(blocks, width, panels),
        ANY,
        [pltpu.VMEM(cells, F32), pltpu.VMEM(cells, BF16), pltpu.VMEM(cells, BF16), pltpu.SemaphoreType.DMA((3, 2 * tile_y))],
        0,
        0,
        "last",
        aliases={3: 0},
    )
    return out.reshape(currents.shape)


def solution(mesh):
    placed = (
        P(("groups", "gx"), "gy", None, None, None),
        P(("groups", "gx"), "gy", None, None, None),
        P(("groups", "gx"), "gy", None, None, None, None),
        P(("groups", "gx"), "gy", None, None),
        P(("groups", "gx"), "gy"),
        P(("groups", "gx"), "gy", None, None, None),
        P(("groups", "gx"), "gy", None, None),
        P(("groups", "gx", "gy"), None, None, None),
        P(("groups", "gx", "gy"), None, None),
        P(("groups", "gx", "gy"), None),
        P(("groups", "gx"), "gy"),
        P("groups"),
    )
    return jax.shard_map(
        per_device,
        mesh=mesh,
        in_specs=placed,
        out_specs=P(("groups", "gx"), "gy", None, None, None),
        check_vma=False,
    )
```

```python
import functools

import jax
import jax.numpy as jnp
from jax import lax
from jax.experimental import pallas as pl
from jax.experimental.pallas import tpu as pltpu
from jax.sharding import PartitionSpec as P

F32 = jnp.float32
BF16 = jnp.bfloat16
GROUP = 4
DEPTH = 3
MIB = 1024 * 1024
VMEM_MIB = {"edges": 8, "leaf": 16, "outward": 54, "fold": 4, "itself": 16, "turn": 12, "near": 46, "far": 26, "last": 8}


def dot_nn(a, b):
    return lax.dot_general(a, b, (((1,), (0,)), ((), ())), preferred_element_type=F32)


def dot_nt(a, b):
    return lax.dot_general(a, b, (((1,), (1,)), ((), ())), preferred_element_type=F32)


def dot_tn(a, b):
    return lax.dot_general(a, b, (((0,), (0,)), ((), ())), preferred_element_type=F32)


def set_pair(win, at, re, im, half):
    panels = re.shape[1]
    win[at, :half, :panels] = re
    win[at, half:, :panels] = im
    win[at, :half, panels:] = -im
    win[at, half:, panels:] = re


def forward(pair, mats):
    return dot_nt(pair, jnp.concatenate([mats[0], mats[1]], axis=1))


def transposed(pair, mats):
    return dot_nn(pair, jnp.concatenate([mats[0], mats[1]], axis=0))


def turned(value, cos, sin, half):
    re = value[:half].astype(F32)
    im = value[half:].astype(F32)
    return cos * re - sin * im, sin * re + cos * im


def cell_phase(bloch, x, y, wide_x, wide_y, panels):
    shift_x = shift_y = 0.0
    if x == 0:
        shift_x = jnp.where(lax.axis_index("gx") == 0, -1.0, 0.0)
    if x == wide_x - 1:
        shift_x = jnp.where(lax.axis_index("gx") == lax.axis_size("gx") - 1, 1.0, 0.0)
    if y == 0:
        shift_y = jnp.where(lax.axis_index("gy") == 0, -1.0, 0.0)
    if y == wide_y - 1:
        shift_y = jnp.where(lax.axis_index("gy") == lax.axis_size("gy") - 1, 1.0, 0.0)
    phase = jnp.full((1, panels), bloch[0] * shift_x + bloch[1] * shift_y, F32)
    return jnp.cos(phase), jnp.sin(phase)


def slot_place(pairs, s, tile_y):
    r = pairs[0, s]
    d = pairs[1, s]
    u = d + jnp.where(d >= 4, 1, 0)
    ux = jnp.where(u >= 6, 2, jnp.where(u >= 3, 1, 0))
    rx = lax.div(r, tile_y)
    ry = r - rx * tile_y
    return r, rx + ux, ry + u - 3 * ux


def list_slots(pairs, count, lists, tile_x, tile_y):
    def one(s, found):
        _, cx, cy = slot_place(pairs, s, tile_y)
        outside = (cx == 0) | (cx == tile_x + 1) | (cy == 0) | (cy == tile_y + 1)
        lists[0, found[0]] = s
        lists[1, found[1]] = s
        step = jnp.where(outside, 1, 0)
        return found[0] + 1 - step, found[1] + step

    zero = jnp.int32(0)
    found = lax.fori_loop(0, count, one, (zero, zero))
    for k in range(2):
        lists[2, k] = found[k]
        for more in range(GROUP):
            lists[k, found[k] + more] = 0


def groups_of(n):
    return lax.div(n + GROUP - 1, GROUP)


def stream(groups, fetch, ring, sems, body):
    def start(g):
        @pl.when(g < groups)
        def _():
            at = lax.rem(g, DEPTH)
            for k in range(GROUP):
                fetch(g * GROUP + k, ring.at[at, k], sems.at[at, k])

    def prime():
        for g in range(DEPTH - 1):
            start(g)

    def step(g, carry):
        at = lax.rem(g, DEPTH)
        for k in range(GROUP):
            pltpu.make_async_copy(ring.at[at, k], ring.at[at, k], sems.at[at, k]).wait()
        start(g + DEPTH - 1)
        body(g, at)
        return carry

    return prime, lambda first, last: lax.fori_loop(first, last, step, 0)


def out_kernel(
    tile_x, tile_y, half, pairs, count, bloch, own, near, left, right, low_corner, high_corner, beside, lists, win, acc, ring,
    sems
):
    blocks = tile_x * tile_y
    wide_x, wide_y = tile_x + 2, tile_y + 2
    panels = own.shape[2]
    list_slots(pairs, count[0, 0], lists, tile_x, tile_y)
    n = lists[2, 1]
    groups = groups_of(n)

    def fetch(t, to, sem):
        pltpu.make_async_copy(near.at[lists[1, t]], to, sem).start()

    def body(g, at):
        for k in range(GROUP):
            t = g * GROUP + k
            r, cx, cy = slot_place(pairs, lists[1, t], tile_y)
            over = jnp.where(cx == 0, 0, wide_y) + cy
            along = 2 * wide_y + jnp.where(cy == 0, 0, tile_x) + cx - 1
            c = jnp.where((cx == 0) | (cx == wide_x - 1), over, along)
            acc[jnp.where(t < n, c, 2 * wide_y + 2 * tile_x)] += transposed(win[r], ring[at, k])

    prime, run = stream(groups, fetch, ring, sems, body)
    prime()
    for b in range(blocks):
        set_pair(win, b, own[b, :half], own[b, half:], half)
    acc[...] = jnp.zeros_like(acc)
    run(0, groups)
    for side in range(2):
        for cy in range(wide_y):
            cos, sin = cell_phase(bloch, (wide_x - 1) * side, cy, wide_x, wide_y, panels)
            re, im = turned(acc.at[side * wide_y + cy], cos, -sin, half)
            if 0 < cy < wide_y - 1:
                row = (left, right)[side]
                row[cy - 1, :half, :] = re.astype(BF16)
                row[cy - 1, half:, :] = im.astype(BF16)
            else:
                corner = (low_corner, high_corner)[side]
                corner[min(cy, 1), :half, :] = re.astype(BF16)
                corner[min(cy, 1), half:, :] = im.astype(BF16)
        for i in range(tile_x):
            cos, sin = cell_phase(bloch, i + 1, (wide_y - 1) * side, wide_x, wide_y, panels)
            re, im = turned(acc.at[2 * wide_y + side * tile_x + i], cos, -sin, half)
            beside[side, i, :half, :] = re.astype(BF16)
            beside[side, i, half:, :] = im.astype(BF16)


def fold_kernel(tile_y, low_corner, high_corner, unused_left, unused_right, left, right, ends, sems):
    del unused_left, unused_right
    steps = []
    for side, row, corner in ((0, left, low_corner), (1, right, high_corner)):
        for end, j in ((0, tile_y - 1), (1, 0)):
            k = 2 * side + end
            get = pltpu.make_async_copy(row.at[j], ends.at[k], sems.at[0, k])
            put = pltpu.make_async_copy(ends.at[k], row.at[j], sems.at[1, k])
            get.start()
            steps.append((get, put, k, corner, end))
    for get, put, k, corner, end in steps:
        get.wait()
        ends[k] = (ends[k].astype(F32) + corner[end].astype(F32)).astype(BF16)
        put.start()
    for _, put, _, _, _ in steps:
        put.wait()


def edge_kernel(tile_x, tile_y, own, first, last, columns, sems):
    blocks = tile_x * tile_y
    puts = [
        pltpu.make_async_copy(own.at[pl.ds(0, tile_y)], first, sems.at[0]),
        pltpu.make_async_copy(own.at[pl.ds(blocks - tile_y, tile_y)], last, sems.at[1]),
    ]
    for i in range(tile_x):
        for side in range(2):
            cell = own.at[i * tile_y + side * (tile_y - 1)]
            puts.append(pltpu.make_async_copy(cell, columns.at[side, i], sems.at[2 + 2 * i + side]))
    for put in puts:
        put.start()
    for put in puts:
        put.wait()


def turn_kernel(rank, bloch, shift, mask, mats, out, flat):
    lanes = flat.shape[1]
    sources = mats.shape[2]
    for p in range(mats.shape[0]):
        phase = bloch[0] * shift[p, 0:1, :].astype(F32) + bloch[1] * shift[p, 1:2, :].astype(F32)
        keep = mask[p : p + 1, :].astype(F32)
        cos, sin = keep * jnp.cos(phase), keep * jnp.sin(phase)
        both = jnp.concatenate([mats[p, 0], mats[p, 1]], axis=0).astype(F32).T
        turn = jnp.concatenate([both[:, sources:], both[:, :sources]], axis=1)
        both = jnp.concatenate([cos, cos], axis=1) * both + jnp.concatenate([-sin, sin], axis=1) * turn
        for at in range(0, 2 * sources, lanes):
            flat[...] = both[:, at : at + lanes]
            for l in range(rank):
                rows = flat[pl.ds(l, rank, stride=rank), :]
                out[l, p * rank : (p + 1) * rank, at : at + lanes] = rows.astype(BF16)


def leaf_kernel(blocks, rank, half, parent, own, basis, moves, unused, coeff, acc):
    del unused
    base = (lax.axis_index("gx") * lax.axis_size("gy") + lax.axis_index("gy")) * acc.shape[0]
    acc[...] = jnp.zeros_like(acc)
    for b in range(blocks):
        raw = dot_nt(basis[b], own[b])
        real = raw[:rank, :half] - raw[rank:, half:]
        imag = raw[:rank, half:] + raw[rank:, :half]
        leaf = jnp.concatenate([real, imag], axis=0)
        high = leaf.astype(BF16)
        low = (leaf - high.astype(F32)).astype(BF16)
        acc[parent[b // parent.shape[1], b % parent.shape[1]] - base] += dot_nn(moves[b], high) + dot_nn(moves[b], low)
    for q in range(acc.shape[0]):
        coeff[q * rank : (q + 1) * rank, :half] = acc[q, :rank].astype(BF16)
        coeff[q * rank : (q + 1) * rank, half:] = acc[q, rank:].astype(BF16)


def self_kernel(blocks, half, own, own_mats, total, win, ring, sems):
    groups = blocks // GROUP

    def fetch(t, to, sem):
        pltpu.make_async_copy(own_mats.at[t], to, sem).start()

    def body(g, at):
        for k in range(GROUP):
            t = g * GROUP + k
            set_pair(win, k, own[t, :half], own[t, half:], half)
        for k in range(GROUP):
            total[g * GROUP + k] = forward(win[k], ring[at, k])

    prime, run = stream(groups, fetch, ring, sems, body)
    prime()
    run(0, groups)


def near_kernel(
    tile_x, tile_y, half, pairs, lists, bloch, own, beside, from_left, from_right, corner, begun, near, total, win, ring, sems,
    begun_sem
):
    blocks = tile_x * tile_y
    wide_x, wide_y = tile_x + 2, tile_y + 2
    panels = own.shape[2]
    n, n_over = lists[2, 0], lists[2, 1]
    begin = pltpu.make_async_copy(begun, total.at[pl.ds(0, blocks)], begun_sem)
    begin.start()
    groups = groups_of(n)
    side_at, over_at = blocks, blocks + 2 * tile_x

    def slot(t):
        return jnp.where(t < groups * GROUP, lists[0, t], lists[1, jnp.maximum(t - groups * GROUP, 0)])

    def fetch(t, to, sem):
        pltpu.make_async_copy(near.at[slot(t)], to, sem).start()

    def body(g, at):
        @pl.when(g < groups)
        def _():
            for k in range(GROUP):
                t = g * GROUP + k
                r, cx, cy = slot_place(pairs, lists[0, t], tile_y)
                live = t < n
                r = jnp.where(live, r, 0)
                c = jnp.where(live, (cx - 1) * tile_y + cy - 1, 0)
                total[jnp.where(live, r, blocks)] += forward(win[c], ring[at, k])
                total[jnp.where(live, c, blocks)] += transposed(win[r], ring[at, k])

        @pl.when(g >= groups)
        def _():
            for k in range(GROUP):
                t = (g - groups) * GROUP + k
                r, cx, cy = slot_place(pairs, lists[1, t], tile_y)
                live = t < n_over
                over = over_at + jnp.where(cx == 0, 0, wide_y) + cy
                c = jnp.where((cx == 0) | (cx == wide_x - 1), over, side_at + jnp.where(cy == 0, 0, tile_x) + cx - 1)
                total[jnp.where(live, r, blocks)] += forward(win[jnp.where(live, c, 0)], ring[at, k])

    every_group = groups + groups_of(n_over)
    prime, run = stream(every_group, fetch, ring, sems, body)
    prime()
    for b in range(blocks):
        set_pair(win, b, own[b, :half], own[b, half:], half)
    for side in range(2):
        for i in range(tile_x):
            cos, sin = cell_phase(bloch, i + 1, side * (wide_y - 1), wide_x, wide_y, panels)
            re, im = turned(beside.at[1 - side, i], cos, sin, half)
            set_pair(win, side_at + side * tile_x + i, re.astype(BF16), im.astype(BF16), half)
        for cy in range(wide_y):
            if cy == 0:
                cell = corner.at[2 * side + 1]
            elif cy == wide_y - 1:
                cell = corner.at[2 * side]
            else:
                cell = (from_left, from_right)[side].at[cy - 1]
            cos, sin = cell_phase(bloch, (wide_x - 1) * side, cy, wide_x, wide_y, panels)
            re, im = turned(cell, cos, sin, half)
            set_pair(win, over_at + side * wide_y + cy, re.astype(BF16), im.astype(BF16), half)
    begin.wait()
    run(0, every_group)


def far_kernel(
    tile_x, tile_y, half, rank, parent, back, coeff, other_low, other_high, coupling, moves, basis, near_total, out, edge, far, gathered,
    stage, out_sem
):
    blocks = tile_x * tile_y
    gx_index, gy_index = lax.axis_index("gx"), lax.axis_index("gy")
    base = (gx_index * lax.axis_size("gy") + gy_index) * far.shape[0]
    rows = far.shape[0] * rank
    middle = coeff.shape[0] // rows // 2
    for first, source, core in ((0, coeff, gy_index), (0, other_low, 1 - gy_index), (middle, other_high, 1 - gy_index)):
        for k in range(first, first + source.shape[0] // rows):
            tile = k * 2 + core
            at = pl.multiple_of(tile * rows, rows)
            for plane in range(2):
                piece = source[(k - first) * rows : (k - first + 1) * rows, plane * half : (plane + 1) * half]
                gathered[plane, pl.ds(at, rows), :] = piece.astype(F32)
    every = gathered.shape[1] // rank
    reals, imags = gathered.at[0], gathered.at[1]
    raw = jnp.zeros((coupling.shape[1], 2 * half), F32)
    for l in range(0, rank, 2):
        terms = []
        for m in (l, l + 1):
            re = reals[pl.ds(m, every, stride=rank), :]
            im = imags[pl.ds(m, every, stride=rank), :]
            terms.append(jnp.concatenate([re, im], axis=1).astype(BF16))
            terms.append(jnp.concatenate([-im, re], axis=1).astype(BF16))
        raw = raw + dot_nn(jnp.concatenate([coupling[l], coupling[l + 1]], axis=1), jnp.concatenate(terms, axis=0))
    for p in range(far.shape[0]):
        far[p, :rank, :] = raw[rank * p : rank * (p + 1), :half]
        far[p, rank:, :] = -raw[rank * p : rank * (p + 1), half:]

    def block(b):
        chosen_far = far[parent[b // tile_y, b % tile_y] - base]
        high = chosen_far.astype(BF16)
        low = (chosen_far - high.astype(F32)).astype(BF16)
        down = (dot_tn(moves[b], high) + dot_tn(moves[b], low)).astype(BF16)
        both = jnp.concatenate([down, jnp.concatenate([-down[rank:], down[:rank]], axis=0)], axis=1)
        value = dot_tn(both, basis[b]) + near_total[b]
        j = b % tile_y
        if j == tile_y - 1:
            value = value + back[0, b // tile_y].astype(F32)
        if j == 0:
            value = value + back[1, b // tile_y].astype(F32)
        return value

    inner = (tile_x - 2) * tile_y
    for b in range(tile_y, blocks - tile_y):
        stage[b - tile_y] = block(b).astype(BF16)
    put = pltpu.make_async_copy(stage, out.at[pl.ds(tile_y, inner)], out_sem)
    put.start()
    for j in range(tile_y):
        edge[j] = block(j)
        edge[tile_y + j] = block(blocks - tile_y + j)
    put.wait()


def last_kernel(tile_x, tile_y, edge, to_first, to_last, unused, out, stage, sems):
    del unused
    blocks = tile_x * tile_y
    puts = []
    for side, came in ((0, to_first), (1, to_last)):
        for j in range(tile_y):
            c = side * tile_y + j
            stage[c] = (edge[c] + came[j].astype(F32)).astype(BF16)
            put = pltpu.make_async_copy(stage.at[c], out.at[j + side * (blocks - tile_y)], sems.at[c])
            put.start()
            puts.append(put)
    for put in puts:
        put.wait()


SMEM = pl.BlockSpec(memory_space=pltpu.SMEM)
VMEM = pl.BlockSpec(memory_space=pltpu.VMEM)
ANY = pl.BlockSpec(memory_space=pl.ANY)


def call(kernel, ins, in_specs, outs, out_specs, scratch, flops, moved, name, aliases=None):
    return pl.pallas_call(
        kernel,
        out_shape=outs,
        in_specs=in_specs,
        out_specs=out_specs,
        scratch_shapes=scratch,
        input_output_aliases=aliases or {},
        compiler_params=pltpu.CompilerParams(vmem_limit_bytes=VMEM_MIB[name] * MIB),
        cost_estimate=pl.CostEstimate(flops=flops // 100, bytes_accessed=moved // 100, transcendentals=0),
        name=name,
    )(*ins)


def per_device(
    currents, self_blocks, near_blocks, near_pairs, near_count, basis, transfer, coupling, far_shift, far_mask, parent, bloch
):
    tile_x, tile_y, _, half, panels = currents.shape
    rank = basis.shape[3]
    blocks = tile_x * tile_y
    wide_x, wide_y = tile_x + 2, tile_y + 2
    gx_count, gy_count = lax.axis_size("gx"), lax.axis_size("gy")
    gx_index, gy_index = lax.axis_index("gx"), lax.axis_index("gy")
    clusters = far_mask.shape[0]
    tiles = gx_count * gy_count
    width = 2 * half
    slots = near_pairs.shape[2]

    def shape(*dims, dtype=BF16):
        return jax.ShapeDtypeStruct(dims, dtype)

    right = [(i, (i + 1) % gx_count) for i in range(gx_count)]
    left = [((i + 1) % gx_count, i) for i in range(gx_count)]
    swap = [(i, (i + 1) % gy_count) for i in range(gy_count)]

    own = currents.reshape(blocks, width, panels)
    pairs = near_pairs.reshape(slots, 2).T
    first, last, columns = call(
        functools.partial(edge_kernel, tile_x, tile_y),
        (own,),
        [VMEM],
        [shape(tile_y, width, panels), shape(tile_y, width, panels), shape(2, tile_x, width, panels)],
        [ANY] * 3,
        [pltpu.SemaphoreType.DMA((2 + 2 * tile_x,))],
        0,
        0,
        "edges",
    )
    from_left = lax.ppermute(last, "gx", right)
    from_right = lax.ppermute(first, "gx", left)
    beside = lax.ppermute(columns, "gy", swap)

    near = near_blocks.reshape(slots, 2, panels, panels)
    own_mats = self_blocks.reshape(blocks, 2, panels, panels)
    basis_b = basis.reshape(blocks, 2 * rank, panels)
    tr = transfer.reshape(blocks, 2, rank, rank)
    moves = jnp.concatenate(
        [jnp.concatenate([tr[:, 0], -tr[:, 1]], axis=2), jnp.concatenate([tr[:, 1], tr[:, 0]], axis=2)], axis=1
    )

    back_left, back_right, low_corner, high_corner, beside_out, lists = call(
        functools.partial(out_kernel, tile_x, tile_y, half),
        (pairs, near_count, bloch, own, near),
        [SMEM, SMEM, SMEM, VMEM, ANY],
        [
            shape(tile_y, width, panels),
            shape(tile_y, width, panels),
            shape(2, width, panels),
            shape(2, width, panels),
            shape(2, tile_x, width, panels),
            shape(3, slots + 2 * GROUP, dtype=jnp.int32),
        ],
        [VMEM] * 5 + [SMEM],
        [
            pltpu.VMEM((blocks, width, 2 * panels), BF16),
            pltpu.VMEM((2 * wide_y + 2 * tile_x + 1, width, panels), F32),
            pltpu.VMEM((DEPTH, GROUP, 2, panels, panels), BF16),
            pltpu.SemaphoreType.DMA((DEPTH, GROUP)),
        ],
        2 * 10 * 2 * width * panels * panels,
        own.size * 2 + 10 * 2 * 2 * panels * panels,
        "outward",
    )
    low_corner = lax.ppermute(low_corner, "gy", swap)
    high_corner = lax.ppermute(high_corner, "gy", swap)
    back = lax.ppermute(beside_out, "gy", swap)
    coeff = call(
        functools.partial(leaf_kernel, blocks, rank, half),
        (parent, own, basis_b, moves, first),
        [SMEM, VMEM, VMEM, VMEM, ANY],
        shape(clusters * rank, width),
        VMEM,
        [pltpu.VMEM((clusters, 2 * rank, half), F32)],
        2 * blocks * 2 * rank * panels * width,
        own.size * 2 + basis_b.size * 2,
        "leaf",
    )
    back_left, back_right = call(
        functools.partial(fold_kernel, tile_y),
        (low_corner, high_corner, back_left, back_right),
        [VMEM, VMEM, ANY, ANY],
        [shape(tile_y, width, panels), shape(tile_y, width, panels)],
        [ANY, ANY],
        [pltpu.VMEM((4, width, panels), BF16), pltpu.SemaphoreType.DMA((2, 4))],
        0,
        0,
        "fold",
        aliases={2: 0, 3: 1},
    )
    to_last = lax.ppermute(back_left, "gx", left)
    to_first = lax.ppermute(back_right, "gx", right)

    self_total = call(
        functools.partial(self_kernel, blocks, half),
        (own, own_mats),
        [VMEM, ANY],
        shape(blocks, width, panels, dtype=F32),
        VMEM,
        [
            pltpu.VMEM((GROUP, width, 2 * panels), BF16),
            pltpu.VMEM((DEPTH, GROUP, 2, panels, panels), BF16),
            pltpu.SemaphoreType.DMA((DEPTH, GROUP)),
        ],
        0,
        0,
        "itself",
    )
    coeff = lax.all_to_all(jnp.broadcast_to(coeff[None], (gx_count,) + coeff.shape), "gx", 0, 0).reshape(-1, width)
    mats = coupling.transpose(0, 2, 1, 3)
    sources = 2 * mats.shape[2]
    mats = call(
        functools.partial(turn_kernel, rank),
        (bloch, far_shift.transpose(0, 2, 1), far_mask, mats),
        [SMEM, VMEM, VMEM, VMEM],
        shape(rank, clusters * rank, sources),
        VMEM,
        [pltpu.VMEM((rank * rank, min(sources, 128)), F32)],
        0,
        0,
        "turn",
    )

    from_left, from_right, _ = lax.optimization_barrier((from_left, from_right, self_total))
    halo_corner = jnp.stack([from_left[0], from_left[tile_y - 1], from_right[0], from_right[tile_y - 1]])
    halo_corner = lax.ppermute(halo_corner, "gy", swap)
    near_total = call(
        functools.partial(near_kernel, tile_x, tile_y, half),
        (pairs, lists, bloch, own, beside, from_left, from_right, halo_corner, self_total, near),
        [SMEM] * 3 + [VMEM] * 5 + [ANY, ANY],
        shape(blocks + 1, width, panels, dtype=F32),
        VMEM,
        [
            pltpu.VMEM((blocks + 2 * tile_x + 2 * wide_y, width, 2 * panels), BF16),
            pltpu.VMEM((DEPTH, GROUP, 2, panels, panels), BF16),
            pltpu.SemaphoreType.DMA((DEPTH, GROUP)),
            pltpu.SemaphoreType.DMA,
        ],
        0,
        0,
        "near",
    )
    coeff, near_total = lax.optimization_barrier((coeff, near_total))
    middle = coeff.shape[0] // 2
    other_low = lax.ppermute(coeff[:middle], "gy", swap)
    other_high = lax.ppermute(coeff[middle:], "gy", swap)

    out, edge = call(
        functools.partial(far_kernel, tile_x, tile_y, half, rank),
        (parent, back, coeff, other_low, other_high, mats, moves, basis_b, near_total),
        [SMEM] + [VMEM] * 8,
        [shape(blocks, width, panels), shape(2 * tile_y, width, panels, dtype=F32)],
        [ANY, VMEM],
        [
            pltpu.VMEM((clusters, 2 * rank, half), F32),
            pltpu.VMEM((2, clusters * tiles * rank, half), F32),
            pltpu.VMEM(((tile_x - 2) * tile_y, width, panels), BF16),
            pltpu.SemaphoreType.DMA,
        ],
        0,
        0,
        "far",
    )
    cells = (2 * tile_y, width, panels)
    out = call(
        functools.partial(last_kernel, tile_x, tile_y),
        (edge, to_first, to_last, out),
        [VMEM, VMEM, VMEM, ANY],
        shape(blocks, width, panels),
        ANY,
        [pltpu.VMEM(cells, BF16), pltpu.SemaphoreType.DMA((2 * tile_y,))],
        0,
        0,
        "last",
        aliases={3: 0},
    )
    return out.reshape(currents.shape)


def solution(mesh):
    placed = (
        P(("groups", "gx"), "gy", None, None, None),
        P(("groups", "gx"), "gy", None, None, None),
        P(("groups", "gx"), "gy", None, None, None, None),
        P(("groups", "gx"), "gy", None, None),
        P(("groups", "gx"), "gy"),
        P(("groups", "gx"), "gy", None, None, None),
        P(("groups", "gx"), "gy", None, None),
        P(("groups", "gx", "gy"), None, None, None),
        P(("groups", "gx", "gy"), None, None),
        P(("groups", "gx", "gy"), None),
        P(("groups", "gx"), "gy"),
        P("groups"),
    )
    return jax.shard_map(
        per_device,
        mesh=mesh,
        in_specs=placed,
        out_specs=P(("groups", "gx"), "gy", None, None, None),
        check_vma=False,
    )
```

```python
import functools

import jax
import jax.numpy as jnp
from jax import lax
from jax.experimental import pallas as pl
from jax.experimental.pallas import tpu as pltpu
from jax.sharding import PartitionSpec as P

F32 = jnp.float32
BF16 = jnp.bfloat16
GROUP = 4
DEPTH = 3
MIB = 1024 * 1024
VMEM_MIB = {"edges": 8, "leaf": 16, "outward": 54, "fold": 4, "turn": 12, "near": 42, "far": 26, "last": 8}


def dot_nn(a, b):
    return lax.dot_general(a, b, (((1,), (0,)), ((), ())), preferred_element_type=F32)


def dot_nt(a, b):
    return lax.dot_general(a, b, (((1,), (1,)), ((), ())), preferred_element_type=F32)


def dot_tn(a, b):
    return lax.dot_general(a, b, (((0,), (0,)), ((), ())), preferred_element_type=F32)


def set_pair(win, at, re, im, half):
    panels = re.shape[1]
    win[at, :half, :panels] = re
    win[at, half:, :panels] = im
    win[at, :half, panels:] = -im
    win[at, half:, panels:] = re


def forward(pair, mats):
    return dot_nt(pair, jnp.concatenate([mats[0], mats[1]], axis=1))


def transposed(pair, mats):
    return dot_nn(pair, jnp.concatenate([mats[0], mats[1]], axis=0))


def turned(value, cos, sin, half):
    re = value[:half].astype(F32)
    im = value[half:].astype(F32)
    return cos * re - sin * im, sin * re + cos * im


def cell_phase(bloch, x, y, wide_x, wide_y, panels):
    shift_x = shift_y = 0.0
    if x == 0:
        shift_x = jnp.where(lax.axis_index("gx") == 0, -1.0, 0.0)
    if x == wide_x - 1:
        shift_x = jnp.where(lax.axis_index("gx") == lax.axis_size("gx") - 1, 1.0, 0.0)
    if y == 0:
        shift_y = jnp.where(lax.axis_index("gy") == 0, -1.0, 0.0)
    if y == wide_y - 1:
        shift_y = jnp.where(lax.axis_index("gy") == lax.axis_size("gy") - 1, 1.0, 0.0)
    phase = jnp.full((1, panels), bloch[0] * shift_x + bloch[1] * shift_y, F32)
    return jnp.cos(phase), jnp.sin(phase)


def slot_place(pairs, s, tile_y):
    r = pairs[0, s]
    d = pairs[1, s]
    u = d + jnp.where(d >= 4, 1, 0)
    ux = jnp.where(u >= 6, 2, jnp.where(u >= 3, 1, 0))
    rx = lax.div(r, tile_y)
    ry = r - rx * tile_y
    return r, rx + ux, ry + u - 3 * ux


def list_slots(pairs, count, lists, tile_x, tile_y):
    def one(s, found):
        _, cx, cy = slot_place(pairs, s, tile_y)
        outside = (cx == 0) | (cx == tile_x + 1) | (cy == 0) | (cy == tile_y + 1)
        lists[0, found[0]] = s
        lists[1, found[1]] = s
        step = jnp.where(outside, 1, 0)
        return found[0] + 1 - step, found[1] + step

    zero = jnp.int32(0)
    found = lax.fori_loop(0, count, one, (zero, zero))
    for k in range(2):
        lists[2, k] = found[k]
        for more in range(GROUP):
            lists[k, found[k] + more] = 0


def groups_of(n):
    return lax.div(n + GROUP - 1, GROUP)


def stream(groups, fetch, ring, sems, body):
    def start(g):
        @pl.when(g < groups)
        def _():
            at = lax.rem(g, DEPTH)
            for k in range(GROUP):
                fetch(g * GROUP + k, ring.at[at, k], sems.at[at, k])

    def prime():
        for g in range(DEPTH - 1):
            start(g)

    def step(g, carry):
        at = lax.rem(g, DEPTH)
        for k in range(GROUP):
            pltpu.make_async_copy(ring.at[at, k], ring.at[at, k], sems.at[at, k]).wait()
        start(g + DEPTH - 1)
        body(g, at)
        return carry

    return prime, lambda first, last: lax.fori_loop(first, last, step, 0)


def out_kernel(
    tile_x, tile_y, half, pairs, count, bloch, own, near, unused, left, right, low_corner, high_corner, beside, lists, win, acc,
    ring, sems
):
    del unused
    blocks = tile_x * tile_y
    wide_x, wide_y = tile_x + 2, tile_y + 2
    panels = own.shape[2]
    list_slots(pairs, count[0, 0], lists, tile_x, tile_y)
    n = lists[2, 1]
    groups = groups_of(n)

    def fetch(t, to, sem):
        pltpu.make_async_copy(near.at[lists[1, t]], to, sem).start()

    def body(g, at):
        for k in range(GROUP):
            t = g * GROUP + k
            r, cx, cy = slot_place(pairs, lists[1, t], tile_y)
            over = jnp.where(cx == 0, 0, wide_y) + cy
            along = 2 * wide_y + jnp.where(cy == 0, 0, tile_x) + cx - 1
            c = jnp.where((cx == 0) | (cx == wide_x - 1), over, along)
            acc[jnp.where(t < n, c, 2 * wide_y + 2 * tile_x)] += transposed(win[r], ring[at, k])

    prime, run = stream(groups, fetch, ring, sems, body)
    prime()
    for b in range(blocks):
        set_pair(win, b, own[b, :half], own[b, half:], half)
    acc[...] = jnp.zeros_like(acc)
    run(0, groups)
    for side in range(2):
        for cy in range(wide_y):
            cos, sin = cell_phase(bloch, (wide_x - 1) * side, cy, wide_x, wide_y, panels)
            re, im = turned(acc.at[side * wide_y + cy], cos, -sin, half)
            if 0 < cy < wide_y - 1:
                row = (left, right)[side]
                row[cy - 1, :half, :] = re.astype(BF16)
                row[cy - 1, half:, :] = im.astype(BF16)
            else:
                corner = (low_corner, high_corner)[side]
                corner[min(cy, 1), :half, :] = re.astype(BF16)
                corner[min(cy, 1), half:, :] = im.astype(BF16)
        for i in range(tile_x):
            cos, sin = cell_phase(bloch, i + 1, (wide_y - 1) * side, wide_x, wide_y, panels)
            re, im = turned(acc.at[2 * wide_y + side * tile_x + i], cos, -sin, half)
            beside[side, i, :half, :] = re.astype(BF16)
            beside[side, i, half:, :] = im.astype(BF16)


def fold_kernel(tile_y, low_corner, high_corner, unused_left, unused_right, left, right, ends, sems):
    del unused_left, unused_right
    steps = []
    for side, row, corner in ((0, left, low_corner), (1, right, high_corner)):
        for end, j in ((0, tile_y - 1), (1, 0)):
            k = 2 * side + end
            get = pltpu.make_async_copy(row.at[j], ends.at[k], sems.at[0, k])
            put = pltpu.make_async_copy(ends.at[k], row.at[j], sems.at[1, k])
            get.start()
            steps.append((get, put, k, corner, end))
    for get, put, k, corner, end in steps:
        get.wait()
        ends[k] = (ends[k].astype(F32) + corner[end].astype(F32)).astype(BF16)
        put.start()
    for _, put, _, _, _ in steps:
        put.wait()


def edge_kernel(tile_x, tile_y, own, first, last, columns, sems):
    blocks = tile_x * tile_y
    puts = [
        pltpu.make_async_copy(own.at[pl.ds(0, tile_y)], first, sems.at[0]),
        pltpu.make_async_copy(own.at[pl.ds(blocks - tile_y, tile_y)], last, sems.at[1]),
    ]
    for i in range(tile_x):
        for side in range(2):
            cell = own.at[i * tile_y + side * (tile_y - 1)]
            puts.append(pltpu.make_async_copy(cell, columns.at[side, i], sems.at[2 + 2 * i + side]))
    for put in puts:
        put.start()
    for put in puts:
        put.wait()


def turn_kernel(rank, bloch, shift, mask, mats, out, flat):
    lanes = flat.shape[1]
    sources = mats.shape[2]
    for p in range(mats.shape[0]):
        phase = bloch[0] * shift[p, 0:1, :].astype(F32) + bloch[1] * shift[p, 1:2, :].astype(F32)
        keep = mask[p : p + 1, :].astype(F32)
        cos, sin = keep * jnp.cos(phase), keep * jnp.sin(phase)
        both = jnp.concatenate([mats[p, 0], mats[p, 1]], axis=0).astype(F32).T
        turn = jnp.concatenate([both[:, sources:], both[:, :sources]], axis=1)
        both = jnp.concatenate([cos, cos], axis=1) * both + jnp.concatenate([-sin, sin], axis=1) * turn
        for at in range(0, 2 * sources, lanes):
            flat[...] = both[:, at : at + lanes]
            for l in range(rank):
                rows = flat[pl.ds(l, rank, stride=rank), :]
                out[l, p * rank : (p + 1) * rank, at : at + lanes] = rows.astype(BF16)


def leaf_kernel(blocks, rank, half, parent, own, basis, moves, unused, coeff, acc):
    del unused
    base = (lax.axis_index("gx") * lax.axis_size("gy") + lax.axis_index("gy")) * acc.shape[0]
    acc[...] = jnp.zeros_like(acc)
    for b in range(blocks):
        raw = dot_nt(basis[b], own[b])
        real = raw[:rank, :half] - raw[rank:, half:]
        imag = raw[:rank, half:] + raw[rank:, :half]
        leaf = jnp.concatenate([real, imag], axis=0)
        high = leaf.astype(BF16)
        low = (leaf - high.astype(F32)).astype(BF16)
        acc[parent[b // parent.shape[1], b % parent.shape[1]] - base] += dot_nn(moves[b], high) + dot_nn(moves[b], low)
    for q in range(acc.shape[0]):
        coeff[q * rank : (q + 1) * rank, :half] = acc[q, :rank].astype(BF16)
        coeff[q * rank : (q + 1) * rank, half:] = acc[q, rank:].astype(BF16)


def near_kernel(
    tile_x, tile_y, half, pairs, lists, bloch, own, beside, from_left, from_right, corner, own_mats, near, total, win, ring, sems
):
    blocks = tile_x * tile_y
    wide_x, wide_y = tile_x + 2, tile_y + 2
    panels = own.shape[2]
    n, n_over = lists[2, 0], lists[2, 1]
    groups = groups_of(n)
    own_groups = blocks // GROUP
    side_at, over_at = blocks, blocks + 2 * tile_x

    def slot(t):
        return jnp.where(t < groups * GROUP, lists[0, t], lists[1, jnp.maximum(t - groups * GROUP, 0)])

    def fetch(t, to, sem):
        @pl.when(t < blocks)
        def _():
            pltpu.make_async_copy(own_mats.at[jnp.minimum(t, blocks - 1)], to, sem).start()

        @pl.when(t >= blocks)
        def _():
            pltpu.make_async_copy(near.at[slot(jnp.maximum(t - blocks, 0))], to, sem).start()

    def body(step, at):
        g = step - own_groups

        @pl.when(g < 0)
        def _():
            for k in range(GROUP):
                t = step * GROUP + k
                total[t] = forward(win[t], ring[at, k])

        @pl.when((g >= 0) & (g < groups))
        def _():
            for k in range(GROUP):
                t = g * GROUP + k
                r, cx, cy = slot_place(pairs, lists[0, t], tile_y)
                live = t < n
                r = jnp.where(live, r, 0)
                c = jnp.where(live, (cx - 1) * tile_y + cy - 1, 0)
                total[jnp.where(live, r, blocks)] += forward(win[c], ring[at, k])
                total[jnp.where(live, c, blocks)] += transposed(win[r], ring[at, k])

        @pl.when(g >= groups)
        def _():
            for k in range(GROUP):
                t = (g - groups) * GROUP + k
                r, cx, cy = slot_place(pairs, lists[1, t], tile_y)
                live = t < n_over
                over = over_at + jnp.where(cx == 0, 0, wide_y) + cy
                c = jnp.where((cx == 0) | (cx == wide_x - 1), over, side_at + jnp.where(cy == 0, 0, tile_x) + cx - 1)
                total[jnp.where(live, r, blocks)] += forward(win[jnp.where(live, c, 0)], ring[at, k])

    every_group = own_groups + groups + groups_of(n_over)
    prime, run = stream(every_group, fetch, ring, sems, body)
    prime()
    for b in range(blocks):
        set_pair(win, b, own[b, :half], own[b, half:], half)
    for side in range(2):
        for i in range(tile_x):
            cos, sin = cell_phase(bloch, i + 1, side * (wide_y - 1), wide_x, wide_y, panels)
            re, im = turned(beside.at[1 - side, i], cos, sin, half)
            set_pair(win, side_at + side * tile_x + i, re.astype(BF16), im.astype(BF16), half)
        for cy in range(wide_y):
            if cy == 0:
                cell = corner.at[2 * side + 1]
            elif cy == wide_y - 1:
                cell = corner.at[2 * side]
            else:
                cell = (from_left, from_right)[side].at[cy - 1]
            cos, sin = cell_phase(bloch, (wide_x - 1) * side, cy, wide_x, wide_y, panels)
            re, im = turned(cell, cos, sin, half)
            set_pair(win, over_at + side * wide_y + cy, re.astype(BF16), im.astype(BF16), half)
    run(0, every_group)


def far_kernel(
    tile_x, tile_y, half, rank, parent, back, coeff, other_low, other_high, coupling, moves, basis, near_total, out, edge, far, gathered,
    stage, out_sem
):
    blocks = tile_x * tile_y
    gx_index, gy_index = lax.axis_index("gx"), lax.axis_index("gy")
    base = (gx_index * lax.axis_size("gy") + gy_index) * far.shape[0]
    rows = far.shape[0] * rank
    middle = coeff.shape[0] // rows // 2
    for first, source, core in ((0, coeff, gy_index), (0, other_low, 1 - gy_index), (middle, other_high, 1 - gy_index)):
        for k in range(first, first + source.shape[0] // rows):
            tile = k * 2 + core
            at = pl.multiple_of(tile * rows, rows)
            for plane in range(2):
                piece = source[(k - first) * rows : (k - first + 1) * rows, plane * half : (plane + 1) * half]
                gathered[plane, pl.ds(at, rows), :] = piece.astype(F32)
    every = gathered.shape[1] // rank
    reals, imags = gathered.at[0], gathered.at[1]
    raw = jnp.zeros((coupling.shape[1], 2 * half), F32)
    for l in range(0, rank, 2):
        terms = []
        for m in (l, l + 1):
            re = reals[pl.ds(m, every, stride=rank), :]
            im = imags[pl.ds(m, every, stride=rank), :]
            terms.append(jnp.concatenate([re, im], axis=1).astype(BF16))
            terms.append(jnp.concatenate([-im, re], axis=1).astype(BF16))
        raw = raw + dot_nn(jnp.concatenate([coupling[l], coupling[l + 1]], axis=1), jnp.concatenate(terms, axis=0))
    for p in range(far.shape[0]):
        far[p, :rank, :] = raw[rank * p : rank * (p + 1), :half]
        far[p, rank:, :] = -raw[rank * p : rank * (p + 1), half:]

    def block(b):
        chosen_far = far[parent[b // tile_y, b % tile_y] - base]
        high = chosen_far.astype(BF16)
        low = (chosen_far - high.astype(F32)).astype(BF16)
        down = (dot_tn(moves[b], high) + dot_tn(moves[b], low)).astype(BF16)
        both = jnp.concatenate([down, jnp.concatenate([-down[rank:], down[:rank]], axis=0)], axis=1)
        value = dot_tn(both, basis[b]) + near_total[b]
        j = b % tile_y
        if j == tile_y - 1:
            value = value + back[0, b // tile_y].astype(F32)
        if j == 0:
            value = value + back[1, b // tile_y].astype(F32)
        return value

    inner = (tile_x - 2) * tile_y
    for b in range(tile_y, blocks - tile_y):
        stage[b - tile_y] = block(b).astype(BF16)
    put = pltpu.make_async_copy(stage, out.at[pl.ds(tile_y, inner)], out_sem)
    put.start()
    for j in range(tile_y):
        edge[j] = block(j)
        edge[tile_y + j] = block(blocks - tile_y + j)
    put.wait()


def last_kernel(tile_x, tile_y, edge, to_first, to_last, unused, out, stage, sems):
    del unused
    blocks = tile_x * tile_y
    puts = []
    for side, came in ((0, to_first), (1, to_last)):
        for j in range(tile_y):
            c = side * tile_y + j
            stage[c] = (edge[c] + came[j].astype(F32)).astype(BF16)
            put = pltpu.make_async_copy(stage.at[c], out.at[j + side * (blocks - tile_y)], sems.at[c])
            put.start()
            puts.append(put)
    for put in puts:
        put.wait()


SMEM = pl.BlockSpec(memory_space=pltpu.SMEM)
VMEM = pl.BlockSpec(memory_space=pltpu.VMEM)
ANY = pl.BlockSpec(memory_space=pl.ANY)


def call(kernel, ins, in_specs, outs, out_specs, scratch, flops, moved, name, aliases=None):
    return pl.pallas_call(
        kernel,
        out_shape=outs,
        in_specs=in_specs,
        out_specs=out_specs,
        scratch_shapes=scratch,
        input_output_aliases=aliases or {},
        compiler_params=pltpu.CompilerParams(vmem_limit_bytes=VMEM_MIB[name] * MIB),
        cost_estimate=pl.CostEstimate(flops=flops // 100, bytes_accessed=moved // 100, transcendentals=0),
        name=name,
    )(*ins)


def per_device(
    currents, self_blocks, near_blocks, near_pairs, near_count, basis, transfer, coupling, far_shift, far_mask, parent, bloch
):
    tile_x, tile_y, _, half, panels = currents.shape
    rank = basis.shape[3]
    blocks = tile_x * tile_y
    wide_x, wide_y = tile_x + 2, tile_y + 2
    gx_count, gy_count = lax.axis_size("gx"), lax.axis_size("gy")
    gx_index, gy_index = lax.axis_index("gx"), lax.axis_index("gy")
    clusters = far_mask.shape[0]
    tiles = gx_count * gy_count
    width = 2 * half
    slots = near_pairs.shape[2]

    def shape(*dims, dtype=BF16):
        return jax.ShapeDtypeStruct(dims, dtype)

    right = [(i, (i + 1) % gx_count) for i in range(gx_count)]
    left = [((i + 1) % gx_count, i) for i in range(gx_count)]
    swap = [(i, (i + 1) % gy_count) for i in range(gy_count)]

    own = currents.reshape(blocks, width, panels)
    pairs = near_pairs.reshape(slots, 2).T
    first, last, columns = call(
        functools.partial(edge_kernel, tile_x, tile_y),
        (own,),
        [VMEM],
        [shape(tile_y, width, panels), shape(tile_y, width, panels), shape(2, tile_x, width, panels)],
        [ANY] * 3,
        [pltpu.SemaphoreType.DMA((2 + 2 * tile_x,))],
        0,
        0,
        "edges",
    )
    from_left = lax.ppermute(last, "gx", right)
    from_right = lax.ppermute(first, "gx", left)
    beside = lax.ppermute(columns, "gy", swap)

    near = near_blocks.reshape(slots, 2, panels, panels)
    own_mats = self_blocks.reshape(blocks, 2, panels, panels)
    basis_b = basis.reshape(blocks, 2 * rank, panels)
    tr = transfer.reshape(blocks, 2, rank, rank)
    moves = jnp.concatenate(
        [jnp.concatenate([tr[:, 0], -tr[:, 1]], axis=2), jnp.concatenate([tr[:, 1], tr[:, 0]], axis=2)], axis=1
    )

    coeff = call(
        functools.partial(leaf_kernel, blocks, rank, half),
        (parent, own, basis_b, moves, first),
        [SMEM, VMEM, VMEM, VMEM, ANY],
        shape(clusters * rank, width),
        VMEM,
        [pltpu.VMEM((clusters, 2 * rank, half), F32)],
        2 * blocks * 2 * rank * panels * width,
        own.size * 2 + basis_b.size * 2,
        "leaf",
    )
    back_left, back_right, low_corner, high_corner, beside_out, lists = call(
        functools.partial(out_kernel, tile_x, tile_y, half),
        (pairs, near_count, bloch, own, near, coeff),
        [SMEM, SMEM, SMEM, VMEM, ANY, ANY],
        [
            shape(tile_y, width, panels),
            shape(tile_y, width, panels),
            shape(2, width, panels),
            shape(2, width, panels),
            shape(2, tile_x, width, panels),
            shape(3, slots + 2 * GROUP, dtype=jnp.int32),
        ],
        [VMEM] * 5 + [SMEM],
        [
            pltpu.VMEM((blocks, width, 2 * panels), BF16),
            pltpu.VMEM((2 * wide_y + 2 * tile_x + 1, width, panels), F32),
            pltpu.VMEM((DEPTH, GROUP, 2, panels, panels), BF16),
            pltpu.SemaphoreType.DMA((DEPTH, GROUP)),
        ],
        2 * 10 * 2 * width * panels * panels,
        own.size * 2 + 10 * 2 * 2 * panels * panels,
        "outward",
    )
    low_corner = lax.ppermute(low_corner, "gy", swap)
    high_corner = lax.ppermute(high_corner, "gy", swap)
    back = lax.ppermute(beside_out, "gy", swap)
    back_left, back_right = call(
        functools.partial(fold_kernel, tile_y),
        (low_corner, high_corner, back_left, back_right),
        [VMEM, VMEM, ANY, ANY],
        [shape(tile_y, width, panels), shape(tile_y, width, panels)],
        [ANY, ANY],
        [pltpu.VMEM((4, width, panels), BF16), pltpu.SemaphoreType.DMA((2, 4))],
        0,
        0,
        "fold",
        aliases={2: 0, 3: 1},
    )
    to_last = lax.ppermute(back_left, "gx", left)
    to_first = lax.ppermute(back_right, "gx", right)

    coeff = lax.all_to_all(jnp.broadcast_to(coeff[None], (gx_count,) + coeff.shape), "gx", 0, 0).reshape(-1, width)
    mats = coupling.transpose(0, 2, 1, 3)
    sources = 2 * mats.shape[2]
    mats = call(
        functools.partial(turn_kernel, rank),
        (bloch, far_shift.transpose(0, 2, 1), far_mask, mats),
        [SMEM, VMEM, VMEM, VMEM],
        shape(rank, clusters * rank, sources),
        VMEM,
        [pltpu.VMEM((rank * rank, min(sources, 128)), F32)],
        0,
        0,
        "turn",
    )

    from_left, from_right, _ = lax.optimization_barrier((from_left, from_right, back_left))
    halo_corner = jnp.stack([from_left[0], from_left[tile_y - 1], from_right[0], from_right[tile_y - 1]])
    halo_corner = lax.ppermute(halo_corner, "gy", swap)
    near_total = call(
        functools.partial(near_kernel, tile_x, tile_y, half),
        (pairs, lists, bloch, own, beside, from_left, from_right, halo_corner, own_mats, near),
        [SMEM] * 3 + [VMEM] * 5 + [ANY, ANY],
        shape(blocks + 1, width, panels, dtype=F32),
        VMEM,
        [
            pltpu.VMEM((blocks + 2 * tile_x + 2 * wide_y, width, 2 * panels), BF16),
            pltpu.VMEM((DEPTH, GROUP, 2, panels, panels), BF16),
            pltpu.SemaphoreType.DMA((DEPTH, GROUP)),
        ],
        0,
        0,
        "near",
    )
    coeff, near_total = lax.optimization_barrier((coeff, near_total))
    middle = coeff.shape[0] // 2
    other_low = lax.ppermute(coeff[:middle], "gy", swap)
    other_high = lax.ppermute(coeff[middle:], "gy", swap)

    out, edge = call(
        functools.partial(far_kernel, tile_x, tile_y, half, rank),
        (parent, back, coeff, other_low, other_high, mats, moves, basis_b, near_total),
        [SMEM] + [VMEM] * 8,
        [shape(blocks, width, panels), shape(2 * tile_y, width, panels, dtype=F32)],
        [ANY, VMEM],
        [
            pltpu.VMEM((clusters, 2 * rank, half), F32),
            pltpu.VMEM((2, clusters * tiles * rank, half), F32),
            pltpu.VMEM(((tile_x - 2) * tile_y, width, panels), BF16),
            pltpu.SemaphoreType.DMA,
        ],
        0,
        0,
        "far",
    )
    cells = (2 * tile_y, width, panels)
    out = call(
        functools.partial(last_kernel, tile_x, tile_y),
        (edge, to_first, to_last, out),
        [VMEM, VMEM, VMEM, ANY],
        shape(blocks, width, panels),
        ANY,
        [pltpu.VMEM(cells, BF16), pltpu.SemaphoreType.DMA((2 * tile_y,))],
        0,
        0,
        "last",
        aliases={3: 0},
    )
    return out.reshape(currents.shape)


def solution(mesh):
    placed = (
        P(("groups", "gx"), "gy", None, None, None),
        P(("groups", "gx"), "gy", None, None, None),
        P(("groups", "gx"), "gy", None, None, None, None),
        P(("groups", "gx"), "gy", None, None),
        P(("groups", "gx"), "gy"),
        P(("groups", "gx"), "gy", None, None, None),
        P(("groups", "gx"), "gy", None, None),
        P(("groups", "gx", "gy"), None, None, None),
        P(("groups", "gx", "gy"), None, None),
        P(("groups", "gx", "gy"), None),
        P(("groups", "gx"), "gy"),
        P("groups"),
    )
    return jax.shard_map(
        per_device,
        mesh=mesh,
        in_specs=placed,
        out_specs=P(("groups", "gx"), "gy", None, None, None),
        check_vma=False,
    )
```

```python
import functools

import jax
import jax.numpy as jnp
from jax import lax
from jax.experimental import pallas as pl
from jax.experimental.pallas import tpu as pltpu
from jax.sharding import PartitionSpec as P

F32 = jnp.float32
BF16 = jnp.bfloat16
GROUP = 4
DEPTH = 3
MIB = 1024 * 1024
VMEM_MIB = {"edges": 8, "leaf": 16, "outward": 54, "fold": 4, "turn": 12, "near": 50, "far": 26, "last": 8}


def dot_nn(a, b):
    return lax.dot_general(a, b, (((1,), (0,)), ((), ())), preferred_element_type=F32)


def dot_nt(a, b):
    return lax.dot_general(a, b, (((1,), (1,)), ((), ())), preferred_element_type=F32)


def dot_tn(a, b):
    return lax.dot_general(a, b, (((0,), (0,)), ((), ())), preferred_element_type=F32)


def set_pair(win, at, re, im, half):
    panels = re.shape[1]
    win[at, :half, :panels] = re
    win[at, half:, :panels] = im
    win[at, :half, panels:] = -im
    win[at, half:, panels:] = re


def forward(pair, mats):
    return dot_nt(pair, jnp.concatenate([mats[0], mats[1]], axis=1))


def transposed(pair, mats):
    return dot_nn(pair, jnp.concatenate([mats[0], mats[1]], axis=0))


def turned(value, cos, sin, half):
    re = value[:half].astype(F32)
    im = value[half:].astype(F32)
    return cos * re - sin * im, sin * re + cos * im


def cell_phase(bloch, x, y, wide_x, wide_y, panels):
    shift_x = shift_y = 0.0
    if x == 0:
        shift_x = jnp.where(lax.axis_index("gx") == 0, -1.0, 0.0)
    if x == wide_x - 1:
        shift_x = jnp.where(lax.axis_index("gx") == lax.axis_size("gx") - 1, 1.0, 0.0)
    if y == 0:
        shift_y = jnp.where(lax.axis_index("gy") == 0, -1.0, 0.0)
    if y == wide_y - 1:
        shift_y = jnp.where(lax.axis_index("gy") == lax.axis_size("gy") - 1, 1.0, 0.0)
    phase = jnp.full((1, panels), bloch[0] * shift_x + bloch[1] * shift_y, F32)
    return jnp.cos(phase), jnp.sin(phase)


def slot_place(pairs, s, tile_y):
    r = pairs[0, s]
    d = pairs[1, s]
    u = d + jnp.where(d >= 4, 1, 0)
    ux = jnp.where(u >= 6, 2, jnp.where(u >= 3, 1, 0))
    rx = lax.div(r, tile_y)
    ry = r - rx * tile_y
    return r, rx + ux, ry + u - 3 * ux


def list_slots(pairs, count, lists, tile_x, tile_y):
    def one(s, found):
        _, cx, cy = slot_place(pairs, s, tile_y)
        outside = (cx == 0) | (cx == tile_x + 1) | (cy == 0) | (cy == tile_y + 1)
        lists[0, found[0]] = s
        lists[1, found[1]] = s
        step = jnp.where(outside, 1, 0)
        return found[0] + 1 - step, found[1] + step

    zero = jnp.int32(0)
    found = lax.fori_loop(0, count, one, (zero, zero))
    for k in range(2):
        lists[2, k] = found[k]
        for more in range(GROUP):
            lists[k, found[k] + more] = 0


def groups_of(n):
    return lax.div(n + GROUP - 1, GROUP)


def stream(groups, fetch, ring, sems, body):
    def start(g):
        @pl.when(g < groups)
        def _():
            at = lax.rem(g, DEPTH)
            for k in range(GROUP):
                fetch(g * GROUP + k, ring.at[at, k], sems.at[at, k])

    def prime():
        for g in range(DEPTH - 1):
            start(g)

    def step(g, carry):
        at = lax.rem(g, DEPTH)
        for k in range(GROUP):
            pltpu.make_async_copy(ring.at[at, k], ring.at[at, k], sems.at[at, k]).wait()
        start(g + DEPTH - 1)
        body(g, at)
        return carry

    return prime, lambda first, last: lax.fori_loop(first, last, step, 0)


def out_kernel(
    tile_x, tile_y, half, pairs, count, bloch, own, near, unused, left, right, low_corner, high_corner, beside, lists, win, acc,
    ring, sems
):
    del unused
    blocks = tile_x * tile_y
    wide_x, wide_y = tile_x + 2, tile_y + 2
    panels = own.shape[2]
    list_slots(pairs, count[0, 0], lists, tile_x, tile_y)
    n = lists[2, 1]
    groups = groups_of(n)

    def fetch(t, to, sem):
        pltpu.make_async_copy(near.at[lists[1, t]], to, sem).start()

    def body(g, at):
        for k in range(GROUP):
            t = g * GROUP + k
            r, cx, cy = slot_place(pairs, lists[1, t], tile_y)
            over = jnp.where(cx == 0, 0, wide_y) + cy
            along = 2 * wide_y + jnp.where(cy == 0, 0, tile_x) + cx - 1
            c = jnp.where((cx == 0) | (cx == wide_x - 1), over, along)
            acc[jnp.where(t < n, c, 2 * wide_y + 2 * tile_x)] += transposed(win[r], ring[at, k])

    prime, run = stream(groups, fetch, ring, sems, body)
    prime()
    for b in range(blocks):
        set_pair(win, b, own[b, :half], own[b, half:], half)
    acc[...] = jnp.zeros_like(acc)
    run(0, groups)
    for side in range(2):
        for cy in range(wide_y):
            cos, sin = cell_phase(bloch, (wide_x - 1) * side, cy, wide_x, wide_y, panels)
            re, im = turned(acc.at[side * wide_y + cy], cos, -sin, half)
            if 0 < cy < wide_y - 1:
                row = (left, right)[side]
                row[cy - 1, :half, :] = re.astype(BF16)
                row[cy - 1, half:, :] = im.astype(BF16)
            else:
                corner = (low_corner, high_corner)[side]
                corner[min(cy, 1), :half, :] = re.astype(BF16)
                corner[min(cy, 1), half:, :] = im.astype(BF16)
        for i in range(tile_x):
            cos, sin = cell_phase(bloch, i + 1, (wide_y - 1) * side, wide_x, wide_y, panels)
            re, im = turned(acc.at[2 * wide_y + side * tile_x + i], cos, -sin, half)
            beside[side, i, :half, :] = re.astype(BF16)
            beside[side, i, half:, :] = im.astype(BF16)


def fold_kernel(tile_y, low_corner, high_corner, unused_left, unused_right, left, right, ends, sems):
    del unused_left, unused_right
    steps = []
    for side, row, corner in ((0, left, low_corner), (1, right, high_corner)):
        for end, j in ((0, tile_y - 1), (1, 0)):
            k = 2 * side + end
            get = pltpu.make_async_copy(row.at[j], ends.at[k], sems.at[0, k])
            put = pltpu.make_async_copy(ends.at[k], row.at[j], sems.at[1, k])
            get.start()
            steps.append((get, put, k, corner, end))
    for get, put, k, corner, end in steps:
        get.wait()
        ends[k] = (ends[k].astype(F32) + corner[end].astype(F32)).astype(BF16)
        put.start()
    for _, put, _, _, _ in steps:
        put.wait()


def edge_kernel(tile_x, tile_y, own, first, last, columns, sems):
    blocks = tile_x * tile_y
    puts = [
        pltpu.make_async_copy(own.at[pl.ds(0, tile_y)], first, sems.at[0]),
        pltpu.make_async_copy(own.at[pl.ds(blocks - tile_y, tile_y)], last, sems.at[1]),
    ]
    for i in range(tile_x):
        for side in range(2):
            cell = own.at[i * tile_y + side * (tile_y - 1)]
            puts.append(pltpu.make_async_copy(cell, columns.at[side, i], sems.at[2 + 2 * i + side]))
    for put in puts:
        put.start()
    for put in puts:
        put.wait()


def turn_kernel(rank, bloch, shift, mask, mats, out, flat):
    lanes = flat.shape[1]
    sources = mats.shape[2]
    for p in range(mats.shape[0]):
        phase = bloch[0] * shift[p, 0:1, :].astype(F32) + bloch[1] * shift[p, 1:2, :].astype(F32)
        keep = mask[p : p + 1, :].astype(F32)
        cos, sin = keep * jnp.cos(phase), keep * jnp.sin(phase)
        both = jnp.concatenate([mats[p, 0], mats[p, 1]], axis=0).astype(F32).T
        turn = jnp.concatenate([both[:, sources:], both[:, :sources]], axis=1)
        both = jnp.concatenate([cos, cos], axis=1) * both + jnp.concatenate([-sin, sin], axis=1) * turn
        for at in range(0, 2 * sources, lanes):
            flat[...] = both[:, at : at + lanes]
            for l in range(rank):
                rows = flat[pl.ds(l, rank, stride=rank), :]
                out[l, p * rank : (p + 1) * rank, at : at + lanes] = rows.astype(BF16)


def leaf_kernel(blocks, rank, half, parent, own, basis, moves, unused, coeff, acc):
    del unused
    base = (lax.axis_index("gx") * lax.axis_size("gy") + lax.axis_index("gy")) * acc.shape[0]
    acc[...] = jnp.zeros_like(acc)
    for b in range(blocks):
        raw = dot_nt(basis[b], own[b])
        real = raw[:rank, :half] - raw[rank:, half:]
        imag = raw[:rank, half:] + raw[rank:, :half]
        leaf = jnp.concatenate([real, imag], axis=0)
        high = leaf.astype(BF16)
        low = (leaf - high.astype(F32)).astype(BF16)
        acc[parent[b // parent.shape[1], b % parent.shape[1]] - base] += dot_nn(moves[b], high) + dot_nn(moves[b], low)
    for q in range(acc.shape[0]):
        coeff[q * rank : (q + 1) * rank, :half] = acc[q, :rank].astype(BF16)
        coeff[q * rank : (q + 1) * rank, half:] = acc[q, rank:].astype(BF16)


def near_kernel(
    tile_x, tile_y, half, pairs, lists, bloch, own, beside, from_left, from_right, corner, own_mats, near, total, win, ring, sems
):
    blocks = tile_x * tile_y
    wide_x, wide_y = tile_x + 2, tile_y + 2
    panels = own.shape[2]
    n, n_over = lists[2, 0], lists[2, 1]
    groups = groups_of(n)
    own_groups = blocks // GROUP
    side_at, over_at = blocks, blocks + 2 * tile_x

    def slot(t):
        return jnp.where(t < groups * GROUP, lists[0, t], lists[1, jnp.maximum(t - groups * GROUP, 0)])

    def fetch(t, to, sem):
        @pl.when(t < blocks)
        def _():
            pltpu.make_async_copy(own_mats.at[jnp.minimum(t, blocks - 1)], to, sem).start()

        @pl.when(t >= blocks)
        def _():
            pltpu.make_async_copy(near.at[slot(jnp.maximum(t - blocks, 0))], to, sem).start()

    def body(step, at):
        g = step - own_groups

        @pl.when(g < 0)
        def _():
            for k in range(GROUP):
                t = step * GROUP + k
                total[t] = forward(win[t], ring[at, k])

        @pl.when((g >= 0) & (g < groups))
        def _():
            for k in range(GROUP):
                t = g * GROUP + k
                r, cx, cy = slot_place(pairs, lists[0, t], tile_y)
                live = t < n
                r = jnp.where(live, r, 0)
                c = jnp.where(live, (cx - 1) * tile_y + cy - 1, 0)
                total[jnp.where(live, r, blocks)] += forward(win[c], ring[at, k])
                total[jnp.where(live, c, blocks)] += transposed(win[r], ring[at, k])

        @pl.when(g >= groups)
        def _():
            for k in range(GROUP):
                t = (g - groups) * GROUP + k
                r, cx, cy = slot_place(pairs, lists[1, t], tile_y)
                live = t < n_over
                over = over_at + jnp.where(cx == 0, 0, wide_y) + cy
                c = jnp.where((cx == 0) | (cx == wide_x - 1), over, side_at + jnp.where(cy == 0, 0, tile_x) + cx - 1)
                total[jnp.where(live, r, blocks)] += forward(win[jnp.where(live, c, 0)], ring[at, k])

    every_group = own_groups + groups + groups_of(n_over)
    prime, run = stream(every_group, fetch, ring, sems, body)
    prime()
    for b in range(blocks):
        set_pair(win, b, own[b, :half], own[b, half:], half)
    for side in range(2):
        for i in range(tile_x):
            cos, sin = cell_phase(bloch, i + 1, side * (wide_y - 1), wide_x, wide_y, panels)
            re, im = turned(beside.at[1 - side, i], cos, sin, half)
            set_pair(win, side_at + side * tile_x + i, re.astype(BF16), im.astype(BF16), half)
        for cy in range(wide_y):
            if cy == 0:
                cell = corner.at[2 * side + 1]
            elif cy == wide_y - 1:
                cell = corner.at[2 * side]
            else:
                cell = (from_left, from_right)[side].at[cy - 1]
            cos, sin = cell_phase(bloch, (wide_x - 1) * side, cy, wide_x, wide_y, panels)
            re, im = turned(cell, cos, sin, half)
            set_pair(win, over_at + side * wide_y + cy, re.astype(BF16), im.astype(BF16), half)
    run(0, every_group)


def far_kernel(
    tile_x, tile_y, half, rank, parent, back, coeff, other_low, other_high, coupling, moves, basis, near_total, out, edge, far, gathered,
    stage, out_sem
):
    blocks = tile_x * tile_y
    gx_index, gy_index = lax.axis_index("gx"), lax.axis_index("gy")
    base = (gx_index * lax.axis_size("gy") + gy_index) * far.shape[0]
    rows = far.shape[0] * rank
    middle = coeff.shape[0] // rows // 2
    for first, source, core in ((0, coeff, gy_index), (0, other_low, 1 - gy_index), (middle, other_high, 1 - gy_index)):
        for k in range(first, first + source.shape[0] // rows):
            tile = k * 2 + core
            at = pl.multiple_of(tile * rows, rows)
            for plane in range(2):
                piece = source[(k - first) * rows : (k - first + 1) * rows, plane * half : (plane + 1) * half]
                gathered[plane, pl.ds(at, rows), :] = piece.astype(F32)
    every = gathered.shape[1] // rank
    reals, imags = gathered.at[0], gathered.at[1]
    raw = jnp.zeros((coupling.shape[1], 2 * half), F32)
    for l in range(0, rank, 2):
        terms = []
        for m in (l, l + 1):
            re = reals[pl.ds(m, every, stride=rank), :]
            im = imags[pl.ds(m, every, stride=rank), :]
            terms.append(jnp.concatenate([re, im], axis=1).astype(BF16))
            terms.append(jnp.concatenate([-im, re], axis=1).astype(BF16))
        raw = raw + dot_nn(jnp.concatenate([coupling[l], coupling[l + 1]], axis=1), jnp.concatenate(terms, axis=0))
    for p in range(far.shape[0]):
        far[p, :rank, :] = raw[rank * p : rank * (p + 1), :half]
        far[p, rank:, :] = -raw[rank * p : rank * (p + 1), half:]

    def block(b):
        chosen_far = far[parent[b // tile_y, b % tile_y] - base]
        high = chosen_far.astype(BF16)
        low = (chosen_far - high.astype(F32)).astype(BF16)
        down = (dot_tn(moves[b], high) + dot_tn(moves[b], low)).astype(BF16)
        both = jnp.concatenate([down, jnp.concatenate([-down[rank:], down[:rank]], axis=0)], axis=1)
        value = dot_tn(both, basis[b]) + near_total[b]
        j = b % tile_y
        if j == tile_y - 1:
            value = value + back[0, b // tile_y].astype(F32)
        if j == 0:
            value = value + back[1, b // tile_y].astype(F32)
        return value

    inner = (tile_x - 2) * tile_y
    for b in range(tile_y, blocks - tile_y):
        stage[b - tile_y] = block(b).astype(BF16)
    put = pltpu.make_async_copy(stage, out.at[pl.ds(tile_y, inner)], out_sem)
    put.start()
    for j in range(tile_y):
        edge[j] = block(j)
        edge[tile_y + j] = block(blocks - tile_y + j)
    put.wait()


def last_kernel(tile_x, tile_y, edge, to_first, to_last, unused, out, stage, sems):
    del unused
    blocks = tile_x * tile_y
    puts = []
    for side, came in ((0, to_first), (1, to_last)):
        for j in range(tile_y):
            c = side * tile_y + j
            stage[c] = (edge[c] + came[j].astype(F32)).astype(BF16)
            put = pltpu.make_async_copy(stage.at[c], out.at[j + side * (blocks - tile_y)], sems.at[c])
            put.start()
            puts.append(put)
    for put in puts:
        put.wait()


SMEM = pl.BlockSpec(memory_space=pltpu.SMEM)
VMEM = pl.BlockSpec(memory_space=pltpu.VMEM)
ANY = pl.BlockSpec(memory_space=pl.ANY)


def call(kernel, ins, in_specs, outs, out_specs, scratch, flops, moved, name, aliases=None):
    return pl.pallas_call(
        kernel,
        out_shape=outs,
        in_specs=in_specs,
        out_specs=out_specs,
        scratch_shapes=scratch,
        input_output_aliases=aliases or {},
        compiler_params=pltpu.CompilerParams(vmem_limit_bytes=VMEM_MIB[name] * MIB),
        cost_estimate=pl.CostEstimate(flops=flops // 100, bytes_accessed=moved // 100, transcendentals=0),
        name=name,
    )(*ins)


def per_device(
    currents, self_blocks, near_blocks, near_pairs, near_count, basis, transfer, coupling, far_shift, far_mask, parent, bloch
):
    tile_x, tile_y, _, half, panels = currents.shape
    rank = basis.shape[3]
    blocks = tile_x * tile_y
    wide_x, wide_y = tile_x + 2, tile_y + 2
    gx_count, gy_count = lax.axis_size("gx"), lax.axis_size("gy")
    gx_index, gy_index = lax.axis_index("gx"), lax.axis_index("gy")
    clusters = far_mask.shape[0]
    tiles = gx_count * gy_count
    width = 2 * half
    slots = near_pairs.shape[2]

    def shape(*dims, dtype=BF16):
        return jax.ShapeDtypeStruct(dims, dtype)

    right = [(i, (i + 1) % gx_count) for i in range(gx_count)]
    left = [((i + 1) % gx_count, i) for i in range(gx_count)]
    swap = [(i, (i + 1) % gy_count) for i in range(gy_count)]

    own = currents.reshape(blocks, width, panels)
    pairs = near_pairs.reshape(slots, 2).T
    first, last, columns = call(
        functools.partial(edge_kernel, tile_x, tile_y),
        (own,),
        [VMEM],
        [shape(tile_y, width, panels), shape(tile_y, width, panels), shape(2, tile_x, width, panels)],
        [ANY] * 3,
        [pltpu.SemaphoreType.DMA((2 + 2 * tile_x,))],
        0,
        0,
        "edges",
    )
    from_left = lax.ppermute(last, "gx", right)
    from_right = lax.ppermute(first, "gx", left)
    beside = lax.ppermute(columns, "gy", swap)

    near = near_blocks.reshape(slots, 2, panels, panels)
    own_mats = self_blocks.reshape(blocks, 2, panels, panels)
    basis_b = basis.reshape(blocks, 2 * rank, panels)
    tr = transfer.reshape(blocks, 2, rank, rank)
    moves = jnp.concatenate(
        [jnp.concatenate([tr[:, 0], -tr[:, 1]], axis=2), jnp.concatenate([tr[:, 1], tr[:, 0]], axis=2)], axis=1
    )

    coeff = call(
        functools.partial(leaf_kernel, blocks, rank, half),
        (parent, own, basis_b, moves, first),
        [SMEM, VMEM, VMEM, VMEM, ANY],
        shape(clusters * rank, width),
        VMEM,
        [pltpu.VMEM((clusters, 2 * rank, half), F32)],
        2 * blocks * 2 * rank * panels * width,
        own.size * 2 + basis_b.size * 2,
        "leaf",
    )
    back_left, back_right, low_corner, high_corner, beside_out, lists = call(
        functools.partial(out_kernel, tile_x, tile_y, half),
        (pairs, near_count, bloch, own, near, coeff),
        [SMEM, SMEM, SMEM, VMEM, ANY, ANY],
        [
            shape(tile_y, width, panels),
            shape(tile_y, width, panels),
            shape(2, width, panels),
            shape(2, width, panels),
            shape(2, tile_x, width, panels),
            shape(3, slots + 2 * GROUP, dtype=jnp.int32),
        ],
        [VMEM] * 5 + [SMEM],
        [
            pltpu.VMEM((blocks, width, 2 * panels), BF16),
            pltpu.VMEM((2 * wide_y + 2 * tile_x + 1, width, panels), F32),
            pltpu.VMEM((DEPTH, GROUP, 2, panels, panels), BF16),
            pltpu.SemaphoreType.DMA((DEPTH, GROUP)),
        ],
        2 * 10 * 2 * width * panels * panels,
        own.size * 2 + 10 * 2 * 2 * panels * panels,
        "outward",
    )
    low_corner = lax.ppermute(low_corner, "gy", swap)
    high_corner = lax.ppermute(high_corner, "gy", swap)
    back = lax.ppermute(beside_out, "gy", swap)
    back_left, back_right = call(
        functools.partial(fold_kernel, tile_y),
        (low_corner, high_corner, back_left, back_right),
        [VMEM, VMEM, ANY, ANY],
        [shape(tile_y, width, panels), shape(tile_y, width, panels)],
        [ANY, ANY],
        [pltpu.VMEM((4, width, panels), BF16), pltpu.SemaphoreType.DMA((2, 4))],
        0,
        0,
        "fold",
        aliases={2: 0, 3: 1},
    )
    to_last = lax.ppermute(back_left, "gx", left)
    to_first = lax.ppermute(back_right, "gx", right)

    coeff = lax.all_to_all(jnp.broadcast_to(coeff[None], (gx_count,) + coeff.shape), "gx", 0, 0).reshape(-1, width)
    mats = coupling.transpose(0, 2, 1, 3)
    sources = 2 * mats.shape[2]
    mats = call(
        functools.partial(turn_kernel, rank),
        (bloch, far_shift.transpose(0, 2, 1), far_mask, mats),
        [SMEM, VMEM, VMEM, VMEM],
        shape(rank, clusters * rank, sources),
        VMEM,
        [pltpu.VMEM((rank * rank, min(sources, 128)), F32)],
        0,
        0,
        "turn",
    )

    from_left, from_right, _ = lax.optimization_barrier((from_left, from_right, back_left))
    halo_corner = jnp.stack([from_left[0], from_left[tile_y - 1], from_right[0], from_right[tile_y - 1]])
    halo_corner = lax.ppermute(halo_corner, "gy", swap)
    near_total = call(
        functools.partial(near_kernel, tile_x, tile_y, half),
        (pairs, lists, bloch, own, beside, from_left, from_right, halo_corner, own_mats, near),
        [SMEM] * 3 + [VMEM] * 5 + [ANY, ANY],
        shape(blocks + 1, width, panels, dtype=F32),
        VMEM,
        [
            pltpu.VMEM((blocks + 2 * tile_x + 2 * wide_y, width, 2 * panels), BF16),
            pltpu.VMEM((DEPTH, GROUP, 2, panels, panels), BF16),
            pltpu.SemaphoreType.DMA((DEPTH, GROUP)),
        ],
        0,
        0,
        "near",
    )
    coeff, near_total = lax.optimization_barrier((coeff, near_total))
    middle = coeff.shape[0] // 2
    other_low = lax.ppermute(coeff[:middle], "gy", swap)
    other_high = lax.ppermute(coeff[middle:], "gy", swap)

    out, edge = call(
        functools.partial(far_kernel, tile_x, tile_y, half, rank),
        (parent, back, coeff, other_low, other_high, mats, moves, basis_b, near_total),
        [SMEM] + [VMEM] * 8,
        [shape(blocks, width, panels), shape(2 * tile_y, width, panels, dtype=F32)],
        [ANY, VMEM],
        [
            pltpu.VMEM((clusters, 2 * rank, half), F32),
            pltpu.VMEM((2, clusters * tiles * rank, half), F32),
            pltpu.VMEM(((tile_x - 2) * tile_y, width, panels), BF16),
            pltpu.SemaphoreType.DMA,
        ],
        0,
        0,
        "far",
    )
    cells = (2 * tile_y, width, panels)
    out = call(
        functools.partial(last_kernel, tile_x, tile_y),
        (edge, to_first, to_last, out),
        [VMEM, VMEM, VMEM, ANY],
        shape(blocks, width, panels),
        ANY,
        [pltpu.VMEM(cells, BF16), pltpu.SemaphoreType.DMA((2 * tile_y,))],
        0,
        0,
        "last",
        aliases={3: 0},
    )
    return out.reshape(currents.shape)


def solution(mesh):
    placed = (
        P(("groups", "gx"), "gy", None, None, None),
        P(("groups", "gx"), "gy", None, None, None),
        P(("groups", "gx"), "gy", None, None, None, None),
        P(("groups", "gx"), "gy", None, None),
        P(("groups", "gx"), "gy"),
        P(("groups", "gx"), "gy", None, None, None),
        P(("groups", "gx"), "gy", None, None),
        P(("groups", "gx", "gy"), None, None, None),
        P(("groups", "gx", "gy"), None, None),
        P(("groups", "gx", "gy"), None),
        P(("groups", "gx"), "gy"),
        P("groups"),
    )
    return jax.shard_map(
        per_device,
        mesh=mesh,
        in_specs=placed,
        out_specs=P(("groups", "gx"), "gy", None, None, None),
        check_vma=False,
    )
```
